32 devices in a mesh: gx: 8 (over z, x), gy: 4 (over y, core).
Axes of the slice: x: 2, y: 2, z: 4, core: 2. Of those that a mesh axis runs over, the one named last changes fastest.
Arguments:
- right_side: float32 [1024, 512], P(('gx', 'gy')), may hold values from -6 to 6
- diagonal: float32 [1024, 512], P(('gx', 'gy')), may hold values from 0.5 to 2
- features: float32 [1024, 64, 512], P(('gx', 'gy')), may hold values from -0.078125 to 0.078125
- neighbours: int32 [1024, 27], P(('gx', 'gy')), may hold values from -1 to 1023, as said below
- vertex_features: float32 [64, 32768], P(None, ('gx', 'gy')), may hold values from -0.75 to 0.75
- vertex_bricks: int32 [32768], P(('gx', 'gy')), may hold values from 0 to 1023, as said below
Outputs:
- solution_field: float32 [1024, 512], P(('gx', 'gy'))
- residual: float32 [1024, 512], P(('gx', 'gy'))
- vertex_values: float32 [32768], P(('gx', 'gy'))
The draws below stay inside these ranges and needn't reach their ends.
Inputs may be any that keep to these rules, and one draw needn't show every extreme that they name: `neighbours`: bricks sit at distinct integer brick coordinates; slot k of a row names the brick at the offset (k // 9 - 1, k // 3 % 3 - 1, k % 3 - 1) from its own, or -1 where no brick is there, so slot 13 names the brick itself and the relation is symmetric. Every brick whose coordinates differ from a brick's by at most two in each direction is held by a device whose gx and gy indices each differ from that brick's holder's by at most one. `vertex_bricks`: vertex n names a brick of its own gx slab: a brick from (n // 4096) * 128 to (n // 4096) * 128 + 127.
All inputs are finite; a program needn't handle non-finite values.
Results may differ from the reference program's by a relative error of at most 0.0002.
Values sent between devices are 32-bit elements; how exact they have to be, the bound alone decides.
A program may use at most 64 MiB of HBM per device.

```python
import math
import jax
import jax.numpy as jnp
from jax import lax

VOX = 512
FEAT = 64
NBR = 27
ITERS = 3
BDEV = 32
NB = 1024
SLAB = 128
NV = 32768
VSLAB = 4096


def draw_neighbours(key, part):
    devices_all = NB // BDEV
    across = SLAB // BDEV
    along = devices_all // across
    cells = 2 * BDEV
    layers = BDEV // 8
    base = jax.random.fold_in(key, 7)

    def choose(device):
        return jax.random.permutation(jax.random.fold_in(base, device), cells)[:BDEV]
    device_ids = jnp.arange(devices_all, dtype=jnp.int32)
    chosen = jax.vmap(choose)(device_ids).astype(jnp.int32)
    occupancy = jnp.full((devices_all, cells), -1, jnp.int32)
    occupancy = occupancy.at[device_ids[:, None], chosen].set(jnp.arange(BDEV, dtype=jnp.int32)[None, :])
    row_of = (device_ids // across)[:, None]
    col_of = (device_ids % across)[:, None]
    pos_x = row_of * 4 + chosen % 4
    pos_y = col_of * 4 + chosen // 4 % 4
    pos_z = chosen // 16
    slots = jnp.arange(NBR, dtype=jnp.int32)
    step_x = slots // 9 - 1
    step_y = slots // 3 % 3 - 1
    step_z = slots % 3 - 1
    target_x = pos_x[:, :, None] + step_x
    target_y = pos_y[:, :, None] + step_y
    target_z = pos_z[:, :, None] + step_z
    inside = (target_x >= 0) & (target_x < along * 4) & (target_y >= 0) & (target_y < across * 4) & (target_z >= 0) & (target_z < layers)
    safe_x = jnp.clip(target_x, 0, along * 4 - 1)
    safe_y = jnp.clip(target_y, 0, across * 4 - 1)
    safe_z = jnp.clip(target_z, 0, layers - 1)
    target_device = safe_x // 4 * across + safe_y // 4
    target_cell = safe_x % 4 + 4 * (safe_y % 4) + 16 * safe_z
    found = occupancy[target_device, target_cell]
    ids = jnp.where(inside & (found >= 0), target_device * BDEV + found, -1)
    return ids.reshape(NB, NBR).astype(jnp.int32)


def draw_vertex_bricks(key, part):
    vertex_ids = jnp.arange(NV, dtype=jnp.int32)
    within = jax.random.randint(jax.random.fold_in(key, 11), (NV,), 0, SLAB, dtype=jnp.int32)
    return (vertex_ids // VSLAB * SLAB + within).astype(jnp.int32)


def shard_levels(stream_key, shape, split, smallest, high):
    factor_of, own = 1.0, jax.random.fold_in(stream_key, 6)
    for dim, parts in split:
        heights = jnp.exp(jax.random.uniform(jax.random.fold_in(own, dim), (parts,), jnp.float32, smallest / len(split), high / len(split)))
        factor_of = factor_of * jnp.repeat(heights, shape[dim] // parts).reshape([-1 if axis == dim else 1 for axis in range(len(shape))])
    return factor_of


def gaussian(rng, shape, scale, reach, split=(), kind=jnp.bfloat16):
    values = scale * jax.random.normal(rng, shape, jnp.float32)
    if split:
        values = values * shard_levels(rng, shape, split, -0.22, 0.18)
    return jnp.clip(values, -reach, reach).astype(kind)


def setup_inputs(seed: int = 0) -> dict:
    seeds = jax.random.split(jax.random.key(seed), 7)
    return {
        "right_side": gaussian(seeds[0], (NB, VOX), 1.0, 6.0, ((0, 32),), jnp.float32),
        "diagonal": jnp.clip(jnp.exp(math.log(2.0) - 1.3862944 * jax.random.uniform(seeds[1], (NB, VOX), jnp.float32) ** shard_levels(seeds[1], (NB, VOX), ((0, 32),), -0.2, 0.2)), 0.5, 2.0),
        "features": gaussian(seeds[2], (NB, FEAT, VOX), (108 * FEAT) ** -0.5, 0.078125, ((0, 32),), jnp.float32),
        "neighbours": draw_neighbours(jax.random.fold_in(seeds[6], 71), 0),
        "vertex_features": gaussian(seeds[4], (FEAT, NV), FEAT ** -0.5, 0.75, ((1, 32),), jnp.float32),
        "vertex_bricks": draw_vertex_bricks(jax.random.fold_in(seeds[6], 71), 0),
    }


def neighbour_sum(values, neighbours):
    valid = neighbours >= 0
    picked = jnp.take(values, jnp.where(valid, neighbours, 0).astype(jnp.int32), axis=0)
    return jnp.sum(jnp.where(valid[:, :, None], picked, jnp.zeros_like(picked)), axis=1)


def coefficient(features, field):
    return jnp.einsum("bfv,bv->bf", features, field, precision=lax.Precision.HIGHEST)


def operate(field, diagonal, features, neighbours):
    first = neighbour_sum(coefficient(features, field), neighbours)
    second = neighbour_sum(first, neighbours)
    return diagonal * field + jnp.einsum("bfv,bf->bv", features, second, precision=lax.Precision.HIGHEST)


def reference(right_side, diagonal, features, neighbours, vertex_features, vertex_bricks):
    solution_field = jnp.zeros_like(right_side)
    residual, direction = right_side, right_side
    norm_now = jnp.sum(residual * residual)
    for step in range(ITERS):
        image = operate(direction, diagonal, features, neighbours)
        alpha = norm_now / jnp.sum(direction * image)
        solution_field = solution_field + alpha * direction
        residual = residual - alpha * image
        norm_next = jnp.sum(residual * residual)
        direction = residual + (norm_next / norm_now) * direction
        norm_now = norm_next
    surface = neighbour_sum(coefficient(features, solution_field), neighbours)
    picked = jnp.take(surface, vertex_bricks.astype(jnp.int32), axis=0)
    vertex_values = jnp.sum(vertex_features * picked.T, axis=0)
    return solution_field, residual, vertex_values
```

```python
import functools

import jax
import jax.numpy as jnp
from jax import lax
from jax.experimental import pallas as pl
from jax.experimental.pallas import tpu as pltpu
from jax.sharding import PartitionSpec as P

ITERS = 3
CHUNKS = 4
MESH = pl.DeviceIdType.MESH
F32 = jnp.float32
BF16 = jnp.bfloat16


def split3(x):
    hi = x.astype(BF16)
    rest = x - hi.astype(F32)
    mid = rest.astype(BF16)
    lo = (rest - mid.astype(F32)).astype(BF16)
    return hi, mid, lo


def iota(shape, dim):
    return lax.broadcasted_iota(jnp.int32, shape, dim)


def kernel(
    along, across, nrows, width, slots,
    b_hbm, d_hbm, f_hbm, nb_ref, vf_hbm, vb_ref,
    x_ref, r_ref, out_ref,
    b_ref, d_ref, f_ref, vf_ref, dr_ref, p_ref, s_ref, w_ref,
    tab, win, slab, sums, nwin, a4, onehot,
    load_sem, tab_send, tab_recv, win_send, win_recv, slab_send, slab_recv, sum_send, sum_recv,
):
    half = nrows // 2
    wrows = 9 * half
    count = along * across
    gx = lax.axis_index("gx")
    gy = lax.axis_index("gy")
    me = gx * across + gy
    log_rows = nrows.bit_length() - 1
    log_across = across.bit_length() - 1

    step = nrows // CHUNKS
    load_b = pltpu.make_async_copy(b_hbm, b_ref, load_sem.at[0])
    load_d = pltpu.make_async_copy(d_hbm, d_ref, load_sem.at[1])
    load_vf = pltpu.make_async_copy(vf_hbm, vf_ref, load_sem.at[2])
    load_f = [
        pltpu.make_async_copy(
            f_hbm.at[pl.ds(c * step, step)], f_ref.at[pl.ds(c * step, step)], load_sem.at[3 + c]
        )
        for c in range(CHUNKS)
    ]
    load_b.start()
    for copy in load_f:
        copy.start()
    load_d.start()
    load_vf.start()

    tab[...] = jnp.full(tab.shape, -1, jnp.int32)
    win[...] = jnp.zeros(win.shape, F32)

    barrier = pltpu.get_barrier_semaphore()

    def peer(p):
        dev = lax.rem(me + p, count)
        return (dev // across, lax.rem(dev, across))

    def over_peers(body):
        if count <= 32:
            for p in range(1, count):
                body(p)
        else:
            def wrapped(p, carry):
                body(p)
                return carry
            lax.fori_loop(1, count, wrapped, 0)

    def greet(p):
        pl.semaphore_signal(barrier, inc=1, device_id=peer(p), device_id_type=MESH)

    over_peers(greet)

    places = []
    for q in range(9):
        if q != 4:
            dx, dy = q // 3 - 1, q % 3 - 1
            there = (gx + dx >= 0) & (gx + dx < along) & (gy + dy >= 0) & (gy + dy < across)
            places.append((q, there, (gx + dx, gy + dy)))

    def halo(buf, send, recv):
        def copy(q, device):
            return pltpu.make_async_remote_copy(
                src_ref=buf.at[4], dst_ref=buf.at[8 - q], send_sem=send.at[q],
                recv_sem=recv.at[8 - q], device_id=device, device_id_type=MESH,
            )

        def arrive(q, device):
            return pltpu.make_async_remote_copy(
                src_ref=buf.at[4], dst_ref=buf.at[q], send_sem=send.at[q],
                recv_sem=recv.at[q], device_id=device, device_id_type=MESH,
            )

        def start():
            for q, there, device in places:
                pl.when(there)(lambda q=q, device=device: copy(q, device).start())

        def wait_recv():
            for q, there, device in places:
                pl.when(there)(lambda q=q, device=device: arrive(q, device).wait_recv())

        def wait_send():
            for q, there, device in places:
                pl.when(there)(lambda q=q, device=device: copy(q, device).wait_send())

        return start, wait_recv, wait_send

    def localize(ids):
        owner = jnp.right_shift(ids, log_rows)
        ox = jnp.right_shift(owner, log_across) - gx + 1
        oy = jnp.bitwise_and(owner, across - 1) - gy + 1
        inside = (ids >= 0) & (ox >= 0) & (ox < 3) & (oy >= 0) & (oy < 3)
        row = jnp.bitwise_and(ids, nrows - 1)
        spot = jnp.where(row >= half, wrows - half, 0) + (ox * 3 + oy) * half + row
        return jnp.where(inside, spot, -1)

    own = nb_ref[...]
    own_t = jnp.transpose(own)
    tab[4, 0:slots, :] = jnp.concatenate([own_t] * (128 // nrows), axis=1)

    pl.semaphore_wait(barrier, count - 1)
    tab_start, tab_wait, tab_done = halo(tab, tab_send, tab_recv)
    tab_start()

    spots = localize(own)
    lanes2 = iota((nrows, wrows), 1)
    n_even = jnp.zeros((nrows, wrows), F32)
    n_odd = jnp.zeros((nrows, wrows), F32)
    for k in range(slots):
        col = spots[:, k:k + 1]
        n_even = jnp.where(col == lanes2, 1.0, n_even)
        n_odd = jnp.where(col == lanes2 + wrows, 1.0, n_odd)
    a4[2 * nrows:3 * nrows, :] = n_even.astype(BF16)
    a4[3 * nrows:4 * nrows, :] = n_odd.astype(BF16)

    load_b.wait()
    lane = iota((width, 128), 1)

    def reduce_coeff(b, rows, acc):
        prod = f_ref[b] * rows
        part = prod[:, 0:128]
        for j in range(1, prod.shape[1] // 128):
            part = part + prod[:, j * 128:(j + 1) * 128]
        total = jnp.sum(part, axis=1, keepdims=True)
        h, i = b // half, b % half
        acc[h] = jnp.where(lane == i, total, acc[h])

    def pack(acc):
        both = jnp.concatenate(acc, axis=0)
        return jnp.transpose(both)[0:half, :]

    acc = [jnp.zeros((width, 128), F32)] * 2
    for c in range(CHUNKS):
        load_f[c].wait()
        for b in range(c * step, (c + 1) * step):
            reduce_coeff(b, b_ref[b:b + 1, :], acc)
    win[0, 4] = pack(acc)
    win_ops = [halo(win.at[k], win_send.at[k], win_recv.at[k]) for k in range(ITERS)]
    win_ops[0][0]()

    vb = vb_ref[...] - gx * (across * nrows)
    vrow = jnp.bitwise_and(vb, nrows - 1)
    code = (
        jnp.where(vrow >= half, across * half - half, 0)
        + jnp.right_shift(vb, log_rows) * half + vrow
    )
    for g in range(across * nrows // 16):
        block = iota((16, vb.shape[1]), 0) + 16 * g
        onehot[16 * g:16 * (g + 1), :] = jnp.where(block == code, 1.0, 0.0).astype(BF16)

    nwin[...] = jnp.zeros(nwin.shape, BF16)
    tab_wait()
    group = iota((slots, 128), 1) // nrows
    for ox in range(3):
        ids = jnp.where(
            group == 0, tab[3 * ox, 0:slots, :],
            jnp.where(group == 1, tab[3 * ox + 1, 0:slots, :], tab[3 * ox + 2, 0:slots, :]),
        )
        target = jnp.where(group < 3, localize(ids), -1)
        rows = [jnp.broadcast_to(target[k:k + 1, :], (16, 128)) for k in range(slots)]
        low, high = ((0, 6), (0, 9), (3, 9))[ox]
        per = (high - low) * half // 16

        def build(g, carry, rows=rows, low=low, per=per, ox=ox):
            h = g // per
            start = pl.multiple_of(h * wrows + low * half + (g - h * per) * 16, 16)
            spot = iota((16, 128), 0) + start
            hits = jnp.zeros((16, 128), F32)
            for row in rows:
                hits = jnp.where(row == spot, 1.0, hits)
            nwin[pl.ds(start, 16), ox * 128:(ox + 1) * 128] = hits.astype(BF16)
            return carry

        lax.fori_loop(0, 2 * per, build, 0)
    n_loc = jnp.concatenate(
        [nwin[4 * half:5 * half, :], nwin[wrows + 4 * half:wrows + 5 * half, :]], axis=0
    )
    for h in range(2):
        two = lax.dot_general(
            n_loc, nwin[h * wrows:(h + 1) * wrows, :], (((1,), (1,)), ((), ())),
            preferred_element_type=F32,
        )
        a4[h * nrows:(h + 1) * nrows, :] = two.astype(BF16)
    load_d.wait()

    low_lanes = iota((nrows, 128), 1) < width
    ar_rows = iota((8, 128), 0)
    ar_lanes = iota((8, 128), 1)

    def fold(x):
        tot = x[0:8, :]
        for i in range(1, x.shape[0] // 8):
            tot = tot + x[8 * i:8 * (i + 1), :]
        res = tot[:, 0:128]
        for j in range(1, x.shape[1] // 128):
            res = res + tot[:, 128 * j:128 * (j + 1)]
        return jnp.sum(res, axis=0, keepdims=True)

    r = b_ref[...]
    beta = None
    firsts = []
    alphas, betas = [], []
    for it in range(ITERS):
        dr = d_ref[...] * r
        dr_ref[...] = dr
        gamma_part = fold(r * r)
        delta_part = fold(r * dr)
        mu_part = fold(r * s_ref[...]) if it else jnp.zeros((1, 128), F32)
        if it == 0:
            win_ops[0][1]()
            cr = win[0].reshape(wrows, 2 * width)
        parts = jnp.concatenate(split3(cr), axis=1)
        prod = jnp.dot(a4[...], parts, preferred_element_type=F32)
        prod = prod[:, 0:128] + prod[:, 128:256] + prod[:, 256:384]
        second = prod[0:nrows] + pltpu.roll(prod[nrows:2 * nrows], width, 1)
        first = prod[2 * nrows:3 * nrows] + pltpu.roll(prod[3 * nrows:], width, 1)
        delta_part = delta_part + fold(jnp.where(low_lanes, first * first, 0.0))
        three = jnp.where(
            ar_rows == 0, gamma_part, jnp.where(ar_rows == 1, delta_part, mu_part)
        )
        three = jnp.sum(three, axis=1, keepdims=True)
        sums[it, me] = jnp.sum(
            jnp.where((ar_rows == ar_lanes) & (ar_rows < 3), three, 0.0), axis=0, keepdims=True
        )

        def send_sum(p, it=it):
            pltpu.make_async_remote_copy(
                src_ref=sums.at[it, me], dst_ref=sums.at[it, me], send_sem=sum_send.at[it],
                recv_sem=sum_recv.at[it], device_id=peer(p), device_id_type=MESH,
            ).start()

        over_peers(send_sum)

        slab[it, gy] = jnp.where(
            low_lanes[0:half], first[0:half], pltpu.roll(first[half:], width, 1)
        )
        for p in range(1, across):
            pltpu.make_async_remote_copy(
                src_ref=slab.at[it, gy], dst_ref=slab.at[it, gy], send_sem=slab_send.at[it],
                recv_sem=slab_recv.at[it], device_id=(gx, lax.rem(gy + p, across)),
                device_id_type=MESH,
            ).start()

        second_t = jnp.transpose(second)[0:width, :]
        acc = [jnp.zeros((width, 128), F32)] * 2
        for b in range(nrows):
            g = jnp.sum(f_ref[b] * second_t[:, b:b + 1], axis=0, keepdims=True)
            row = dr_ref[b:b + 1, :] + g
            w_ref[b:b + 1, :] = row
            if it < ITERS - 1:
                reduce_coeff(b, row, acc)
        if it < ITERS - 1:
            win[it + 1, 4] = pack(acc)
            win_ops[it + 1][0]()
        else:
            load_vf.wait()
            for k in range(ITERS):
                pltpu.make_async_copy(
                    slab.at[k, pl.ds(0, across - 1)], slab.at[k, pl.ds(0, across - 1)],
                    slab_recv.at[k],
                ).wait()
            pieces = [slab[k].reshape(across * half, 2 * width) for k in range(ITERS)]
            old = pieces[1] + betas[1] * pieces[0]
            known = alphas[0] * pieces[0] + alphas[1] * old
            vert = []
            for piece in (known, pieces[2], old):
                turned = jnp.transpose(piece)
                turned = jnp.concatenate([turned[0:width], turned[width:]], axis=1)
                hi = turned.astype(BF16)
                lo = (turned - hi.astype(F32)).astype(BF16)
                both = jnp.dot(
                    jnp.concatenate([hi, lo], axis=0), onehot[...], preferred_element_type=F32
                )
                vert.append(jnp.sum(
                    (both[0:width] + both[width:]) * vf_ref[...], axis=0, keepdims=True
                ))

        pltpu.make_async_copy(
            sums.at[it, pl.ds(0, count - 1)], sums.at[it, pl.ds(0, count - 1)], sum_recv.at[it]
        ).wait()
        total = jnp.sum(sums[it], axis=0)
        gamma, delta, mu = total[:, 0:1], total[:, 1:2], total[:, 2:3]
        if it == 0:
            energy = delta
        else:
            beta = gamma / gamma_old
            energy = delta + beta * (2.0 * mu + beta * energy)
        alpha = gamma / energy
        gamma_old = gamma
        alphas.append(alpha)
        betas.append(beta)
        if it < ITERS - 1:
            win_ops[it + 1][1]()
            cw = win[it + 1].reshape(wrows, 2 * width)
            cs = cw if it == 0 else cw + beta * cs
            cr = cr - alpha * cs
        w = w_ref[...]
        if it == 0:
            p, s = r, w
            x = alpha * p
        else:
            p = r + beta * p_ref[...]
            s = w + beta * s_ref[...]
            x = x_ref[...] + alpha * p
        r = r - alpha * s
        x_ref[...] = x
        if it < ITERS - 1:
            p_ref[...] = p
            s_ref[...] = s
    r_ref[...] = r
    out_ref[...] = vert[0] + alphas[2] * (vert[1] + betas[2] * vert[2])

    tab_done()
    for it in range(ITERS):
        win_ops[it][2]()
        pltpu.make_async_copy(
            sums.at[it, pl.ds(0, count - 1)], sums.at[it, pl.ds(0, count - 1)], sum_send.at[it]
        ).wait()
        pltpu.make_async_copy(
            slab.at[it, pl.ds(0, across - 1)], slab.at[it, pl.ds(0, across - 1)],
            slab_send.at[it],
        ).wait()


def per_device(right_side, diagonal, features, neighbours, vertex_features, vertex_bricks):
    nrows, width, vox = features.shape
    slots = neighbours.shape[1]
    verts = vertex_bricks.shape[0]
    along, across = lax.axis_size("gx"), lax.axis_size("gy")
    count = along * across
    half = nrows // 2
    any_spec = pl.BlockSpec(memory_space=pl.ANY)
    vmem = pl.BlockSpec(memory_space=pltpu.VMEM)
    field = jax.ShapeDtypeStruct((nrows, vox), F32)
    x, r, out = pl.pallas_call(
        functools.partial(kernel, along, across, nrows, width, slots),
        out_shape=(field, field, jax.ShapeDtypeStruct((1, verts), F32)),
        in_specs=[any_spec, any_spec, any_spec, vmem, any_spec, vmem],
        out_specs=(vmem, vmem, vmem),
        scratch_shapes=[
            pltpu.VMEM((nrows, vox), F32),
            pltpu.VMEM((nrows, vox), F32),
            pltpu.VMEM((nrows, width, vox), F32),
            pltpu.VMEM((width, verts), F32),
            pltpu.VMEM((nrows, vox), F32),
            pltpu.VMEM((nrows, vox), F32),
            pltpu.VMEM((nrows, vox), F32),
            pltpu.VMEM((nrows, vox), F32),
            pltpu.VMEM((9, 32, 128), jnp.int32),
            pltpu.VMEM((ITERS, 9, half, 2 * width), F32),
            pltpu.VMEM((ITERS, across, half, 2 * width), F32),
            pltpu.VMEM((ITERS, count, 1, 128), F32),
            pltpu.VMEM((9 * nrows, 384), BF16),
            pltpu.VMEM((4 * nrows, 9 * half), BF16),
            pltpu.VMEM((across * nrows, verts), BF16),
            pltpu.SemaphoreType.DMA((3 + CHUNKS,)),
            pltpu.SemaphoreType.DMA((9,)),
            pltpu.SemaphoreType.DMA((9,)),
            pltpu.SemaphoreType.DMA((ITERS, 9)),
            pltpu.SemaphoreType.DMA((ITERS, 9)),
            pltpu.SemaphoreType.DMA((ITERS,)),
            pltpu.SemaphoreType.DMA((ITERS,)),
            pltpu.SemaphoreType.DMA((ITERS,)),
            pltpu.SemaphoreType.DMA((ITERS,)),
        ],
        compiler_params=pltpu.CompilerParams(
            collective_id=0, has_side_effects=True, vmem_limit_bytes=40 * 1024 * 1024
        ),
    )(right_side, diagonal, features, neighbours, vertex_features, vertex_bricks.reshape(1, verts))
    return x, r, out.reshape(verts)


def solution(mesh):
    rows = P(("gx", "gy"), None)
    placed = (rows, rows, P(("gx", "gy"), None, None), rows, P(None, ("gx", "gy")), P(("gx", "gy")))
    return jax.shard_map(
        per_device,
        mesh=mesh,
        in_specs=placed,
        out_specs=(rows, rows, P(("gx", "gy"))),
        check_vma=False,
    )
```

```python
import functools

import jax
import jax.numpy as jnp
from jax import lax
from jax.experimental import pallas as pl
from jax.experimental.pallas import tpu as pltpu
from jax.sharding import PartitionSpec as P

ITERS = 3
CHUNKS = 4
VMEM_BYTES = 64 * 1024 * 1024
MESH = pl.DeviceIdType.MESH
F32 = jnp.float32
BF16 = jnp.bfloat16


def split3(x):
    hi = x.astype(BF16)
    rest = x - hi.astype(F32)
    mid = rest.astype(BF16)
    lo = (rest - mid.astype(F32)).astype(BF16)
    return hi, mid, lo


def iota(shape, dim):
    return lax.broadcasted_iota(jnp.int32, shape, dim)


def kernel(
    along, across, nrows, width, slots,
    b_hbm, d_hbm, f_hbm, nb_hbm, vf_hbm, vb_hbm,
    x_hbm, r_hbm, out_hbm,
    x_ref, r_ref, out_ref, b_ref, d_ref, f_ref, nb_ref, vf_ref, vb_ref, dr_ref, p_ref, s_ref, w_ref,
    tab, win, slab, sums, nwin, a4, onehot,
    load_sem, store_sem, tab_send, tab_recv, win_send, win_recv, slab_send, slab_recv, sum_send, sum_recv,
):
    half = nrows // 2
    wrows = 9 * half
    count = along * across
    gx = lax.axis_index("gx")
    gy = lax.axis_index("gy")
    me = gx * across + gy
    log_rows = nrows.bit_length() - 1
    log_across = across.bit_length() - 1

    step = nrows // CHUNKS
    load_b = pltpu.make_async_copy(b_hbm, b_ref, load_sem.at[0])
    load_d = pltpu.make_async_copy(d_hbm, d_ref, load_sem.at[1])
    load_vf = pltpu.make_async_copy(vf_hbm, vf_ref, load_sem.at[2])
    load_f = [
        pltpu.make_async_copy(
            f_hbm.at[pl.ds(c * step, step)], f_ref.at[pl.ds(c * step, step)], load_sem.at[5 + c]
        )
        for c in range(CHUNKS)
    ]
    load_nb = pltpu.make_async_copy(nb_hbm, nb_ref, load_sem.at[3])
    load_vb = pltpu.make_async_copy(vb_hbm, vb_ref, load_sem.at[4])
    load_nb.start()
    load_b.start()
    load_vb.start()
    for copy in load_f:
        copy.start()
    load_d.start()
    load_vf.start()

    tab[...] = jnp.full(tab.shape, -1, jnp.int32)
    win[...] = jnp.zeros(win.shape, F32)

    barrier = pltpu.get_barrier_semaphore()

    def peer(p):
        dev = lax.rem(me + p, count)
        return (dev // across, lax.rem(dev, across))

    def over_peers(body):
        if count <= 32:
            for p in range(1, count):
                body(p)
        else:
            def wrapped(p, carry):
                body(p)
                return carry
            lax.fori_loop(1, count, wrapped, 0)

    def greet(p):
        pl.semaphore_signal(barrier, inc=1, device_id=peer(p), device_id_type=MESH)

    over_peers(greet)

    places = []
    for q in range(9):
        if q != 4:
            dx, dy = q // 3 - 1, q % 3 - 1
            there = (gx + dx >= 0) & (gx + dx < along) & (gy + dy >= 0) & (gy + dy < across)
            places.append((q, there, (gx + dx, gy + dy)))

    def halo(buf, send, recv):
        def copy(q, device):
            return pltpu.make_async_remote_copy(
                src_ref=buf.at[4], dst_ref=buf.at[8 - q], send_sem=send.at[q],
                recv_sem=recv.at[8 - q], device_id=device, device_id_type=MESH,
            )

        def arrive(q, device):
            return pltpu.make_async_remote_copy(
                src_ref=buf.at[4], dst_ref=buf.at[q], send_sem=send.at[q],
                recv_sem=recv.at[q], device_id=device, device_id_type=MESH,
            )

        def start():
            for q, there, device in places:
                pl.when(there)(lambda q=q, device=device: copy(q, device).start())

        def wait_recv():
            for q, there, device in places:
                pl.when(there)(lambda q=q, device=device: arrive(q, device).wait_recv())

        def wait_send():
            for q, there, device in places:
                pl.when(there)(lambda q=q, device=device: copy(q, device).wait_send())

        return start, wait_recv, wait_send

    def localize(ids):
        owner = jnp.right_shift(ids, log_rows)
        ox = jnp.right_shift(owner, log_across) - gx + 1
        oy = jnp.bitwise_and(owner, across - 1) - gy + 1
        inside = (ids >= 0) & (ox >= 0) & (ox < 3) & (oy >= 0) & (oy < 3)
        row = jnp.bitwise_and(ids, nrows - 1)
        spot = jnp.where(row >= half, wrows - half, 0) + (ox * 3 + oy) * half + row
        return jnp.where(inside, spot, -1)

    load_nb.wait()
    own = nb_ref[...]
    own_t = jnp.transpose(own)
    tab[4, 0:slots, :] = jnp.concatenate([own_t] * (128 // nrows), axis=1)

    spots = localize(own)
    lanes2 = iota((nrows, wrows), 1)
    n_even = jnp.zeros((nrows, wrows), F32)
    n_odd = jnp.zeros((nrows, wrows), F32)
    for k in range(slots):
        col = spots[:, k:k + 1]
        n_even = jnp.where(col == lanes2, 1.0, n_even)
        n_odd = jnp.where(col == lanes2 + wrows, 1.0, n_odd)
    a4[2 * nrows:3 * nrows, :] = n_even.astype(BF16)
    a4[3 * nrows:4 * nrows, :] = n_odd.astype(BF16)

    load_vb.wait()
    vb = vb_ref[...] - gx * (across * nrows)
    vrow = jnp.bitwise_and(vb, nrows - 1)
    code = (
        jnp.where(vrow >= half, across * half - half, 0)
        + jnp.right_shift(vb, log_rows) * half + vrow
    )
    for g in range(across * nrows // 16):
        block = iota((16, vb.shape[1]), 0) + 16 * g
        onehot[16 * g:16 * (g + 1), :] = jnp.where(block == code, 1.0, 0.0).astype(BF16)

    nwin[...] = jnp.zeros(nwin.shape, BF16)

    pl.semaphore_wait(barrier, count - 1)
    tab_start, tab_wait, tab_done = halo(tab, tab_send, tab_recv)
    tab_start()

    load_b.wait()
    lane = iota((width, 128), 1)

    def reduce_coeff(b, rows, acc):
        prod = f_ref[b] * rows
        part = prod[:, 0:128]
        for j in range(1, prod.shape[1] // 128):
            part = part + prod[:, j * 128:(j + 1) * 128]
        total = jnp.sum(part, axis=1, keepdims=True)
        h, i = b // half, b % half
        acc[h] = jnp.where(lane == i, total, acc[h])

    def pack(acc):
        both = jnp.concatenate(acc, axis=0)
        return jnp.transpose(both)[0:half, :]

    acc = [jnp.zeros((width, 128), F32)] * 2
    for c in range(CHUNKS):
        load_f[c].wait()
        for b in range(c * step, (c + 1) * step):
            reduce_coeff(b, b_ref[b:b + 1, :], acc)
    win[0, 4] = pack(acc)
    win_ops = [halo(win.at[k], win_send.at[k], win_recv.at[k]) for k in range(ITERS)]
    win_ops[0][0]()

    tab_wait()
    group = iota((slots, 128), 1) // nrows
    for ox in range(3):
        ids = jnp.where(
            group == 0, tab[3 * ox, 0:slots, :],
            jnp.where(group == 1, tab[3 * ox + 1, 0:slots, :], tab[3 * ox + 2, 0:slots, :]),
        )
        target = jnp.where(group < 3, localize(ids), -1)
        rows = [jnp.broadcast_to(target[k:k + 1, :], (16, 128)) for k in range(slots)]
        low, high = ((0, 6), (0, 9), (3, 9))[ox]
        per = (high - low) * half // 16

        def build(g, carry, rows=rows, low=low, per=per, ox=ox):
            h = g // per
            start = pl.multiple_of(h * wrows + low * half + (g - h * per) * 16, 16)
            spot = iota((16, 128), 0) + start
            hits = jnp.zeros((16, 128), F32)
            for row in rows:
                hits = jnp.where(row == spot, 1.0, hits)
            nwin[pl.ds(start, 16), ox * 128:(ox + 1) * 128] = hits.astype(BF16)
            return carry

        lax.fori_loop(0, 2 * per, build, 0)
    n_loc = jnp.concatenate(
        [nwin[4 * half:5 * half, :], nwin[wrows + 4 * half:wrows + 5 * half, :]], axis=0
    )
    for h in range(2):
        two = lax.dot_general(
            n_loc, nwin[h * wrows:(h + 1) * wrows, :], (((1,), (1,)), ((), ())),
            preferred_element_type=F32,
        )
        a4[h * nrows:(h + 1) * nrows, :] = two.astype(BF16)
    load_d.wait()

    low_lanes = iota((nrows, 128), 1) < width
    ar_rows = iota((8, 128), 0)
    ar_lanes = iota((8, 128), 1)

    def fold(x):
        tot = x[0:8, :]
        for i in range(1, x.shape[0] // 8):
            tot = tot + x[8 * i:8 * (i + 1), :]
        res = tot[:, 0:128]
        for j in range(1, x.shape[1] // 128):
            res = res + tot[:, 128 * j:128 * (j + 1)]
        return jnp.sum(res, axis=0, keepdims=True)

    r = b_ref[...]
    beta = None
    firsts = []
    alphas, betas = [], []
    for it in range(ITERS):
        dr = d_ref[...] * r
        dr_ref[...] = dr
        gamma_part = fold(r * r)
        delta_part = fold(r * dr)
        mu_part = fold(r * s_ref[...]) if it else jnp.zeros((1, 128), F32)
        if it == 0:
            win_ops[0][1]()
            cr = win[0].reshape(wrows, 2 * width)
        parts = jnp.concatenate(split3(cr), axis=1)
        prod = jnp.dot(a4[...], parts, preferred_element_type=F32)
        prod = prod[:, 0:128] + prod[:, 128:256] + prod[:, 256:384]
        second = prod[0:nrows] + pltpu.roll(prod[nrows:2 * nrows], width, 1)
        first = prod[2 * nrows:3 * nrows] + pltpu.roll(prod[3 * nrows:], width, 1)
        delta_part = delta_part + fold(jnp.where(low_lanes, first * first, 0.0))
        three = jnp.where(
            ar_rows == 0, gamma_part, jnp.where(ar_rows == 1, delta_part, mu_part)
        )
        three = jnp.sum(three, axis=1, keepdims=True)
        sums[it, me] = jnp.sum(
            jnp.where((ar_rows == ar_lanes) & (ar_rows < 3), three, 0.0), axis=0, keepdims=True
        )

        def send_sum(p, it=it):
            pltpu.make_async_remote_copy(
                src_ref=sums.at[it, me], dst_ref=sums.at[it, me], send_sem=sum_send.at[it],
                recv_sem=sum_recv.at[it], device_id=peer(p), device_id_type=MESH,
            ).start()

        over_peers(send_sum)

        slab[it, gy] = jnp.where(
            low_lanes[0:half], first[0:half], pltpu.roll(first[half:], width, 1)
        )
        for p in range(1, across):
            pltpu.make_async_remote_copy(
                src_ref=slab.at[it, gy], dst_ref=slab.at[it, gy], send_sem=slab_send.at[it],
                recv_sem=slab_recv.at[it], device_id=(gx, lax.rem(gy + p, across)),
                device_id_type=MESH,
            ).start()

        second_t = jnp.transpose(second)[0:width, :]
        acc = [jnp.zeros((width, 128), F32)] * 2
        for b in range(nrows):
            g = jnp.sum(f_ref[b] * second_t[:, b:b + 1], axis=0, keepdims=True)
            row = dr_ref[b:b + 1, :] + g
            w_ref[b:b + 1, :] = row
            if it < ITERS - 1:
                reduce_coeff(b, row, acc)
        if it < ITERS - 1:
            win[it + 1, 4] = pack(acc)
            win_ops[it + 1][0]()
        else:
            load_vf.wait()
            for k in range(ITERS):
                pltpu.make_async_copy(
                    slab.at[k, pl.ds(0, across - 1)], slab.at[k, pl.ds(0, across - 1)],
                    slab_recv.at[k],
                ).wait()
            pieces = [slab[k].reshape(across * half, 2 * width) for k in range(ITERS)]
            old = pieces[1] + betas[1] * pieces[0]
            known = alphas[0] * pieces[0] + alphas[1] * old
            vert = []
            for piece in (known, pieces[2], old):
                turned = jnp.transpose(piece)
                turned = jnp.concatenate([turned[0:width], turned[width:]], axis=1)
                hi = turned.astype(BF16)
                lo = (turned - hi.astype(F32)).astype(BF16)
                both = jnp.dot(
                    jnp.concatenate([hi, lo], axis=0), onehot[...], preferred_element_type=F32
                )
                vert.append(jnp.sum(
                    (both[0:width] + both[width:]) * vf_ref[...], axis=0, keepdims=True
                ))

        pltpu.make_async_copy(
            sums.at[it, pl.ds(0, count - 1)], sums.at[it, pl.ds(0, count - 1)], sum_recv.at[it]
        ).wait()
        total = jnp.sum(sums[it], axis=0)
        gamma, delta, mu = total[:, 0:1], total[:, 1:2], total[:, 2:3]
        if it == 0:
            energy = delta
        else:
            beta = gamma / gamma_old
            energy = delta + beta * (2.0 * mu + beta * energy)
        alpha = gamma / energy
        gamma_old = gamma
        alphas.append(alpha)
        betas.append(beta)
        if it < ITERS - 1:
            win_ops[it + 1][1]()
            cw = win[it + 1].reshape(wrows, 2 * width)
            cs = cw if it == 0 else cw + beta * cs
            cr = cr - alpha * cs
        w = w_ref[...]
        if it == 0:
            p, s = r, w
            x = alpha * p
        else:
            p = r + beta * p_ref[...]
            s = w + beta * s_ref[...]
            x = x_ref[...] + alpha * p
        r = r - alpha * s
        x_ref[...] = x
        if it < ITERS - 1:
            p_ref[...] = p
            s_ref[...] = s
    r_ref[...] = r
    stores = [
        pltpu.make_async_copy(a, b, store_sem.at[i])
        for i, (a, b) in enumerate(((x_ref, x_hbm), (r_ref, r_hbm), (out_ref, out_hbm)))
    ]
    stores[0].start()
    stores[1].start()
    out_ref[...] = vert[0] + alphas[2] * (vert[1] + betas[2] * vert[2])

    stores[2].start()

    tab_done()
    for it in range(ITERS):
        win_ops[it][2]()
        pltpu.make_async_copy(
            sums.at[it, pl.ds(0, count - 1)], sums.at[it, pl.ds(0, count - 1)], sum_send.at[it]
        ).wait()
        pltpu.make_async_copy(
            slab.at[it, pl.ds(0, across - 1)], slab.at[it, pl.ds(0, across - 1)],
            slab_send.at[it],
        ).wait()
    for copy in stores:
        copy.wait()


def finish(x_in, r_in, v_in, x_out, r_out, v_out, sems):
    copies = [
        pltpu.make_async_copy(a, b, sems.at[i])
        for i, (a, b) in enumerate(((x_in, x_out), (r_in, r_out), (v_in, v_out)))
    ]
    for copy in copies:
        copy.start()
    for copy in copies:
        copy.wait()


def per_device(right_side, diagonal, features, neighbours, vertex_features, vertex_bricks):
    nrows, width, vox = features.shape
    slots = neighbours.shape[1]
    verts = vertex_bricks.shape[0]
    along, across = lax.axis_size("gx"), lax.axis_size("gy")
    count = along * across
    half = nrows // 2
    hbm = pl.BlockSpec(memory_space=pltpu.HBM)
    field = jax.ShapeDtypeStruct((nrows, vox), F32)
    x, r, out = pl.pallas_call(
        functools.partial(kernel, along, across, nrows, width, slots),
        out_shape=(field, field, jax.ShapeDtypeStruct((1, verts), F32)),
        in_specs=[hbm] * 6,
        out_specs=[hbm] * 3,
        scratch_shapes=[
            pltpu.VMEM((nrows, vox), F32),
            pltpu.VMEM((nrows, vox), F32),
            pltpu.VMEM((1, verts), F32),
            pltpu.VMEM((nrows, vox), F32),
            pltpu.VMEM((nrows, vox), F32),
            pltpu.VMEM((nrows, width, vox), F32),
            pltpu.VMEM((nrows, slots), jnp.int32),
            pltpu.VMEM((width, verts), F32),
            pltpu.VMEM((1, verts), jnp.int32),
            pltpu.VMEM((nrows, vox), F32),
            pltpu.VMEM((nrows, vox), F32),
            pltpu.VMEM((nrows, vox), F32),
            pltpu.VMEM((nrows, vox), F32),
            pltpu.VMEM((9, 32, 128), jnp.int32),
            pltpu.VMEM((ITERS, 9, half, 2 * width), F32),
            pltpu.VMEM((ITERS, across, half, 2 * width), F32),
            pltpu.VMEM((ITERS, count, 1, 128), F32),
            pltpu.VMEM((9 * nrows, 384), BF16),
            pltpu.VMEM((4 * nrows, 9 * half), BF16),
            pltpu.VMEM((across * nrows, verts), BF16),
            pltpu.SemaphoreType.DMA((5 + CHUNKS,)),
            pltpu.SemaphoreType.DMA((3,)),
            pltpu.SemaphoreType.DMA((9,)),
            pltpu.SemaphoreType.DMA((9,)),
            pltpu.SemaphoreType.DMA((ITERS, 9)),
            pltpu.SemaphoreType.DMA((ITERS, 9)),
            pltpu.SemaphoreType.DMA((ITERS,)),
            pltpu.SemaphoreType.DMA((ITERS,)),
            pltpu.SemaphoreType.DMA((ITERS,)),
            pltpu.SemaphoreType.DMA((ITERS,)),
        ],
        compiler_params=pltpu.CompilerParams(
            collective_id=0, has_side_effects=True, vmem_limit_bytes=VMEM_BYTES
        ),
    )(right_side, diagonal, features, neighbours, vertex_features, vertex_bricks.reshape(1, verts))
    x, r, out = pl.pallas_call(
        finish,
        out_shape=(field, field, jax.ShapeDtypeStruct((1, verts), F32)),
        in_specs=[hbm] * 3,
        out_specs=[hbm] * 3,
        scratch_shapes=[pltpu.SemaphoreType.DMA((3,))],
        compiler_params=pltpu.CompilerParams(vmem_limit_bytes=VMEM_BYTES),
    )(x, r, out)
    return x, r, out.reshape(verts)


def solution(mesh):
    rows = P(("gx", "gy"), None)
    placed = (rows, rows, P(("gx", "gy"), None, None), rows, P(None, ("gx", "gy")), P(("gx", "gy")))
    return jax.shard_map(
        per_device,
        mesh=mesh,
        in_specs=placed,
        out_specs=(rows, rows, P(("gx", "gy"))),
        check_vma=False,
    )
```

```python
import functools

import jax
import jax.numpy as jnp
from jax import lax
from jax.experimental import pallas as pl
from jax.experimental.pallas import tpu as pltpu
from jax.sharding import PartitionSpec as P

ITERS = 3
CHUNKS = 4
VMEM_BYTES = 64 * 1024 * 1024
MESH = pl.DeviceIdType.MESH
F32 = jnp.float32
BF16 = jnp.bfloat16


def split3(x):
    hi = x.astype(BF16)
    rest = x - hi.astype(F32)
    mid = rest.astype(BF16)
    lo = (rest - mid.astype(F32)).astype(BF16)
    return hi, mid, lo


def iota(shape, dim):
    return lax.broadcasted_iota(jnp.int32, shape, dim)


def kernel(
    along, across, nrows, width, slots,
    b_hbm, d_hbm, f_hbm, nb_hbm, vf_hbm, vb_hbm,
    x_ref, r_ref, out_ref,
    b_ref, d_ref, f_ref, nb_ref, vf_ref, vb_ref, dr_ref, p_ref, s_ref, w_ref,
    tab, win, slab, row_sums, col_sums, nwin, a4, onehot,
    load_sem, tab_send, tab_recv, win_send, win_recv, slab_send, slab_recv,
    row_send, row_recv, col_send, col_recv,
):
    half = nrows // 2
    wrows = 9 * half
    gx = lax.axis_index("gx")
    gy = lax.axis_index("gy")
    log_rows = nrows.bit_length() - 1
    log_across = across.bit_length() - 1

    step = nrows // CHUNKS
    load_b = pltpu.make_async_copy(b_hbm, b_ref, load_sem.at[0])
    load_d = pltpu.make_async_copy(d_hbm, d_ref, load_sem.at[1])
    load_vf = pltpu.make_async_copy(vf_hbm, vf_ref, load_sem.at[2])
    load_f = [
        pltpu.make_async_copy(
            f_hbm.at[pl.ds(c * step, step)], f_ref.at[pl.ds(c * step, step)], load_sem.at[5 + c]
        )
        for c in range(CHUNKS)
    ]
    load_nb = pltpu.make_async_copy(nb_hbm, nb_ref, load_sem.at[3])
    load_vb = pltpu.make_async_copy(vb_hbm, vb_ref, load_sem.at[4])
    load_nb.start()
    load_b.start()
    load_vb.start()
    for copy in load_f:
        copy.start()
    load_d.start()
    load_vf.start()

    tab[...] = jnp.full(tab.shape, -1, jnp.int32)
    win[...] = jnp.zeros(win.shape, F32)

    barrier = pltpu.get_barrier_semaphore()
    row_peers = [(gx, lax.rem(gy + p, across)) for p in range(1, across)]
    col_peers = [(lax.rem(gx + p, along), gy) for p in range(1, along)]
    corners = [
        (lax.rem(gx + dx, along), lax.rem(gy + dy, across))
        for dx in (1, along - 1) for dy in (1, across - 1)
    ]
    partners = row_peers + col_peers + corners
    for device in partners:
        pl.semaphore_signal(barrier, inc=1, device_id=device, device_id_type=MESH)

    places = []
    for q in range(9):
        if q != 4:
            dx, dy = q // 3 - 1, q % 3 - 1
            there = (gx + dx >= 0) & (gx + dx < along) & (gy + dy >= 0) & (gy + dy < across)
            places.append((q, there, (gx + dx, gy + dy)))

    def halo(buf, send, recv):
        def copy(q, device):
            return pltpu.make_async_remote_copy(
                src_ref=buf.at[4], dst_ref=buf.at[8 - q], send_sem=send.at[q],
                recv_sem=recv.at[8 - q], device_id=device, device_id_type=MESH,
            )

        def arrive(q, device):
            return pltpu.make_async_remote_copy(
                src_ref=buf.at[4], dst_ref=buf.at[q], send_sem=send.at[q],
                recv_sem=recv.at[q], device_id=device, device_id_type=MESH,
            )

        def start():
            for q, there, device in places:
                pl.when(there)(lambda q=q, device=device: copy(q, device).start())

        def wait_recv():
            for q, there, device in places:
                pl.when(there)(lambda q=q, device=device: arrive(q, device).wait_recv())

        def wait_send():
            for q, there, device in places:
                pl.when(there)(lambda q=q, device=device: copy(q, device).wait_send())

        return start, wait_recv, wait_send

    def localize(ids):
        owner = jnp.right_shift(ids, log_rows)
        ox = jnp.right_shift(owner, log_across) - gx + 1
        oy = jnp.bitwise_and(owner, across - 1) - gy + 1
        inside = (ids >= 0) & (ox >= 0) & (ox < 3) & (oy >= 0) & (oy < 3)
        row = jnp.bitwise_and(ids, nrows - 1)
        spot = jnp.where(row >= half, wrows - half, 0) + (ox * 3 + oy) * half + row
        return jnp.where(inside, spot, -1)

    load_nb.wait()
    own = nb_ref[...]
    own_t = jnp.transpose(own)
    tab[4, 0:slots, :] = jnp.concatenate([own_t] * (128 // nrows), axis=1)

    spots = localize(own)
    lanes2 = iota((nrows, wrows), 1)
    n_even = jnp.zeros((nrows, wrows), F32)
    n_odd = jnp.zeros((nrows, wrows), F32)
    for k in range(slots):
        col = spots[:, k:k + 1]
        n_even = jnp.where(col == lanes2, 1.0, n_even)
        n_odd = jnp.where(col == lanes2 + wrows, 1.0, n_odd)
    a4[2 * nrows:3 * nrows, :] = n_even.astype(BF16)
    a4[3 * nrows:4 * nrows, :] = n_odd.astype(BF16)

    load_vb.wait()
    vb = vb_ref[...] - gx * (across * nrows)
    vrow = jnp.bitwise_and(vb, nrows - 1)
    code = (
        jnp.where(vrow >= half, across * half - half, 0)
        + jnp.right_shift(vb, log_rows) * half + vrow
    )
    for g in range(across * nrows // 16):
        block = iota((16, vb.shape[1]), 0) + 16 * g
        onehot[16 * g:16 * (g + 1), :] = jnp.where(block == code, 1.0, 0.0).astype(BF16)

    nwin[...] = jnp.zeros(nwin.shape, BF16)

    pl.semaphore_wait(barrier, len(partners))
    tab_start, tab_wait, tab_done = halo(tab, tab_send, tab_recv)
    tab_start()

    load_b.wait()
    lane = iota((width, 128), 1)

    def reduce_coeff(b, rows, acc):
        prod = f_ref[b] * rows
        part = prod[:, 0:128]
        for j in range(1, prod.shape[1] // 128):
            part = part + prod[:, j * 128:(j + 1) * 128]
        total = jnp.sum(part, axis=1, keepdims=True)
        h, i = b // half, b % half
        acc[h] = jnp.where(lane == i, total, acc[h])

    def pack(acc):
        both = jnp.concatenate(acc, axis=0)
        return jnp.transpose(both)[0:half, :]

    acc = [jnp.zeros((width, 128), F32)] * 2
    for c in range(CHUNKS):
        load_f[c].wait()
        for b in range(c * step, (c + 1) * step):
            reduce_coeff(b, b_ref[b:b + 1, :], acc)
    win[0, 4] = pack(acc)
    win_ops = [halo(win.at[k], win_send.at[k], win_recv.at[k]) for k in range(ITERS)]
    win_ops[0][0]()

    tab_wait()
    group = iota((slots, 128), 1) // nrows
    for ox in range(3):
        ids = jnp.where(
            group == 0, tab[3 * ox, 0:slots, :],
            jnp.where(group == 1, tab[3 * ox + 1, 0:slots, :], tab[3 * ox + 2, 0:slots, :]),
        )
        target = jnp.where(group < 3, localize(ids), -1)
        rows = [jnp.broadcast_to(target[k:k + 1, :], (16, 128)) for k in range(slots)]
        low, high = ((0, 6), (0, 9), (3, 9))[ox]
        per = (high - low) * half // 16

        def build(g, carry, rows=rows, low=low, per=per, ox=ox):
            h = g // per
            start = pl.multiple_of(h * wrows + low * half + (g - h * per) * 16, 16)
            spot = iota((16, 128), 0) + start
            hits = jnp.zeros((16, 128), F32)
            for row in rows:
                hits = jnp.where(row == spot, 1.0, hits)
            nwin[pl.ds(start, 16), ox * 128:(ox + 1) * 128] = hits.astype(BF16)
            return carry

        lax.fori_loop(0, 2 * per, build, 0)
    n_loc = jnp.concatenate(
        [nwin[4 * half:5 * half, :], nwin[wrows + 4 * half:wrows + 5 * half, :]], axis=0
    )
    for h in range(2):
        two = lax.dot_general(
            n_loc, nwin[h * wrows:(h + 1) * wrows, :], (((1,), (1,)), ((), ())),
            preferred_element_type=F32,
        )
        a4[h * nrows:(h + 1) * nrows, :] = two.astype(BF16)
    load_d.wait()

    low_lanes = iota((nrows, 128), 1) < width
    ar_rows = iota((8, 128), 0)
    ar_lanes = iota((8, 128), 1)

    def fold(x):
        tot = x[0:8, :]
        for i in range(1, x.shape[0] // 8):
            tot = tot + x[8 * i:8 * (i + 1), :]
        res = tot[:, 0:128]
        for j in range(1, x.shape[1] // 128):
            res = res + tot[:, 128 * j:128 * (j + 1)]
        return jnp.sum(res, axis=0, keepdims=True)

    def spread(buf, own, send, recv, peers):
        for device in peers:
            pltpu.make_async_remote_copy(
                src_ref=buf.at[it, own], dst_ref=buf.at[it, own], send_sem=send.at[it],
                recv_sem=recv.at[it], device_id=device, device_id_type=MESH,
            ).start()

    def landed(buf, k, sem, number):
        part = buf.at[k, pl.ds(0, number)]
        pltpu.make_async_copy(part, part, sem.at[k]).wait()

    def second_stage():
        landed(row_sums, it, row_recv, across - 1)
        col_sums[it, gx] = jnp.sum(row_sums[it], axis=0)
        spread(col_sums, gx, col_send, col_recv, col_peers)

    r = b_ref[...]
    beta = None
    firsts = []
    alphas, betas = [], []
    for it in range(ITERS):
        dr = d_ref[...] * r
        dr_ref[...] = dr
        gamma_part = fold(r * r)
        delta_part = fold(r * dr)
        mu_part = fold(r * s_ref[...]) if it else jnp.zeros((1, 128), F32)
        if it == 0:
            win_ops[0][1]()
            cr = win[0].reshape(wrows, 2 * width)
        parts = jnp.concatenate(split3(cr), axis=1)
        prod = jnp.dot(a4[...], parts, preferred_element_type=F32)
        prod = prod[:, 0:128] + prod[:, 128:256] + prod[:, 256:384]
        second = prod[0:nrows] + pltpu.roll(prod[nrows:2 * nrows], width, 1)
        first = prod[2 * nrows:3 * nrows] + pltpu.roll(prod[3 * nrows:], width, 1)
        delta_part = delta_part + fold(jnp.where(low_lanes, first * first, 0.0))
        three = jnp.where(
            ar_rows == 0, gamma_part, jnp.where(ar_rows == 1, delta_part, mu_part)
        )
        three = jnp.sum(three, axis=1, keepdims=True)
        row_sums[it, gy] = jnp.sum(
            jnp.where((ar_rows == ar_lanes) & (ar_rows < 3), three, 0.0), axis=0, keepdims=True
        )

        spread(row_sums, gy, row_send, row_recv, row_peers)

        slab[it, gy] = jnp.where(
            low_lanes[0:half], first[0:half], pltpu.roll(first[half:], width, 1)
        )
        spread(slab, gy, slab_send, slab_recv, row_peers)

        second_t = jnp.transpose(second)[0:width, :]
        acc = [jnp.zeros((width, 128), F32)] * 2
        for b in range(nrows):
            if it < ITERS - 1 and b == nrows * 3 // 4:
                second_stage()
            g = jnp.sum(f_ref[b] * second_t[:, b:b + 1], axis=0, keepdims=True)
            row = dr_ref[b:b + 1, :] + g
            w_ref[b:b + 1, :] = row
            if it < ITERS - 1:
                reduce_coeff(b, row, acc)
        if it < ITERS - 1:
            win[it + 1, 4] = pack(acc)
            win_ops[it + 1][0]()
        else:
            second_stage()
            load_vf.wait()
            for k in range(ITERS):
                landed(slab, k, slab_recv, across - 1)
            pieces = [slab[k].reshape(across * half, 2 * width) for k in range(ITERS)]
            old = pieces[1] + betas[1] * pieces[0]
            known = alphas[0] * pieces[0] + alphas[1] * old
            vert = []
            for piece in (known, pieces[2], old):
                turned = jnp.transpose(piece)
                turned = jnp.concatenate([turned[0:width], turned[width:]], axis=1)
                hi = turned.astype(BF16)
                lo = (turned - hi.astype(F32)).astype(BF16)
                both = jnp.dot(
                    jnp.concatenate([hi, lo], axis=0), onehot[...], preferred_element_type=F32
                )
                vert.append(jnp.sum(
                    (both[0:width] + both[width:]) * vf_ref[...], axis=0, keepdims=True
                ))

        landed(col_sums, it, col_recv, along - 1)
        total = jnp.sum(col_sums[it], axis=0)
        gamma, delta, mu = total[:, 0:1], total[:, 1:2], total[:, 2:3]
        if it == 0:
            energy = delta
        else:
            beta = gamma / gamma_old
            energy = delta + beta * (2.0 * mu + beta * energy)
        alpha = gamma / energy
        gamma_old = gamma
        alphas.append(alpha)
        betas.append(beta)
        if it < ITERS - 1:
            win_ops[it + 1][1]()
            cw = win[it + 1].reshape(wrows, 2 * width)
            cs = cw if it == 0 else cw + beta * cs
            cr = cr - alpha * cs
        w = w_ref[...]
        if it == 0:
            p, s = r, w
            x = alpha * p
        else:
            p = r + beta * p_ref[...]
            s = w + beta * s_ref[...]
            x = x_ref[...] + alpha * p
        r = r - alpha * s
        x_ref[...] = x
        if it < ITERS - 1:
            p_ref[...] = p
            s_ref[...] = s
    r_ref[...] = r
    out_ref[...] = vert[0] + alphas[2] * (vert[1] + betas[2] * vert[2])


    tab_done()
    for it in range(ITERS):
        win_ops[it][2]()
        landed(row_sums, it, row_send, across - 1)
        landed(col_sums, it, col_send, along - 1)
        landed(slab, it, slab_send, across - 1)


def finish(x_in, r_in, v_in, x_out, r_out, v_out, sems):
    copies = [
        pltpu.make_async_copy(a, b, sems.at[i])
        for i, (a, b) in enumerate(((x_in, x_out), (r_in, r_out), (v_in, v_out)))
    ]
    for copy in copies:
        copy.start()
    for copy in copies:
        copy.wait()


def per_device(right_side, diagonal, features, neighbours, vertex_features, vertex_bricks):
    nrows, width, vox = features.shape
    slots = neighbours.shape[1]
    verts = vertex_bricks.shape[0]
    along, across = lax.axis_size("gx"), lax.axis_size("gy")
    half = nrows // 2
    vmem = pl.BlockSpec(memory_space=pltpu.VMEM)
    hbm = pl.BlockSpec(memory_space=pltpu.HBM)
    field = jax.ShapeDtypeStruct((nrows, vox), F32)
    x, r, out = pl.pallas_call(
        functools.partial(kernel, along, across, nrows, width, slots),
        out_shape=(field, field, jax.ShapeDtypeStruct((1, verts), F32)),
        in_specs=[hbm] * 6,
        out_specs=[vmem] * 3,
        scratch_shapes=[
            pltpu.VMEM((nrows, vox), F32),
            pltpu.VMEM((nrows, vox), F32),
            pltpu.VMEM((nrows, width, vox), F32),
            pltpu.VMEM((nrows, slots), jnp.int32),
            pltpu.VMEM((width, verts), F32),
            pltpu.VMEM((1, verts), jnp.int32),
            pltpu.VMEM((nrows, vox), F32),
            pltpu.VMEM((nrows, vox), F32),
            pltpu.VMEM((nrows, vox), F32),
            pltpu.VMEM((nrows, vox), F32),
            pltpu.VMEM((9, 32, 128), jnp.int32),
            pltpu.VMEM((ITERS, 9, half, 2 * width), F32),
            pltpu.VMEM((ITERS, across, half, 2 * width), F32),
            pltpu.VMEM((ITERS, across, 1, 128), F32),
            pltpu.VMEM((ITERS, along, 1, 128), F32),
            pltpu.VMEM((9 * nrows, 384), BF16),
            pltpu.VMEM((4 * nrows, 9 * half), BF16),
            pltpu.VMEM((across * nrows, verts), BF16),
            pltpu.SemaphoreType.DMA((5 + CHUNKS,)),
            pltpu.SemaphoreType.DMA((9,)),
            pltpu.SemaphoreType.DMA((9,)),
            pltpu.SemaphoreType.DMA((ITERS, 9)),
            pltpu.SemaphoreType.DMA((ITERS, 9)),
            pltpu.SemaphoreType.DMA((ITERS,)),
            pltpu.SemaphoreType.DMA((ITERS,)),
            pltpu.SemaphoreType.DMA((ITERS,)),
            pltpu.SemaphoreType.DMA((ITERS,)),
            pltpu.SemaphoreType.DMA((ITERS,)),
            pltpu.SemaphoreType.DMA((ITERS,)),
        ],
        compiler_params=pltpu.CompilerParams(
            collective_id=0, has_side_effects=True, vmem_limit_bytes=VMEM_BYTES
        ),
    )(right_side, diagonal, features, neighbours, vertex_features, vertex_bricks.reshape(1, verts))
    x, r, out = pl.pallas_call(
        finish,
        out_shape=(field, field, jax.ShapeDtypeStruct((1, verts), F32)),
        in_specs=[vmem] * 3,
        out_specs=[hbm] * 3,
        scratch_shapes=[pltpu.SemaphoreType.DMA((3,))],
        compiler_params=pltpu.CompilerParams(vmem_limit_bytes=VMEM_BYTES),
    )(x, r, out)
    return x, r, out.reshape(verts)


def solution(mesh):
    rows = P(("gx", "gy"), None)
    placed = (rows, rows, P(("gx", "gy"), None, None), rows, P(None, ("gx", "gy")), P(("gx", "gy")))
    return jax.shard_map(
        per_device,
        mesh=mesh,
        in_specs=placed,
        out_specs=(rows, rows, P(("gx", "gy"))),
        check_vma=False,
    )
```

```python
import functools

import jax
import jax.numpy as jnp
from jax import lax
from jax.experimental import pallas as pl
from jax.experimental.pallas import tpu as pltpu
from jax.sharding import PartitionSpec as P

ITERS = 3
CHUNKS = 4
VMEM_BYTES = 64 * 1024 * 1024
MESH = pl.DeviceIdType.MESH
F32 = jnp.float32
BF16 = jnp.bfloat16


def split3(x):
    hi = x.astype(BF16)
    rest = x - hi.astype(F32)
    mid = rest.astype(BF16)
    lo = (rest - mid.astype(F32)).astype(BF16)
    return hi, mid, lo


def iota(shape, dim):
    return lax.broadcasted_iota(jnp.int32, shape, dim)


def kernel(
    along, across, nrows, width, slots,
    b_hbm, d_hbm, f_hbm, nb_hbm, vf_hbm, vb_hbm,
    x_ref, r_ref, out_ref,
    b_ref, d_ref, f_ref, nb_ref, vf_ref, vb_ref, dr_ref, p_ref, s_ref, w_ref,
    tab, win, slab, sums, nwin, a4, onehot, spread_sel, rep,
    load_sem, tab_send, tab_recv, win_send, win_recv, slab_send, slab_recv,
    sum_send, sum_recv,
):
    half = nrows // 2
    wrows = 9 * half
    count = along * across
    gx = lax.axis_index("gx")
    gy = lax.axis_index("gy")
    me = gx * across + gy
    log_rows = nrows.bit_length() - 1
    log_across = across.bit_length() - 1

    step = nrows // CHUNKS
    load_b = pltpu.make_async_copy(b_hbm, b_ref, load_sem.at[0])
    load_d = pltpu.make_async_copy(d_hbm, d_ref, load_sem.at[1])
    load_vf = pltpu.make_async_copy(vf_hbm, vf_ref, load_sem.at[2])
    load_f = [
        pltpu.make_async_copy(
            f_hbm.at[pl.ds(c * step, step)], f_ref.at[pl.ds(c * step, step)], load_sem.at[5 + c]
        )
        for c in range(CHUNKS)
    ]
    load_nb = pltpu.make_async_copy(nb_hbm, nb_ref, load_sem.at[3])
    load_vb = pltpu.make_async_copy(vb_hbm, vb_ref, load_sem.at[4])
    load_nb.start()
    load_b.start()
    load_vb.start()
    for copy in load_f:
        copy.start()
    load_d.start()
    load_vf.start()

    tab[...] = jnp.full(tab.shape, -1, jnp.int32)
    win[...] = jnp.zeros(win.shape, F32)

    barrier = pltpu.get_barrier_semaphore()
    row_peers = [(gx, lax.rem(gy + p, across)) for p in range(1, across)]

    def peer(p):
        dev = lax.rem(me + p, count)
        return (dev // across, lax.rem(dev, across))

    def over_peers(body):
        if count <= 32:
            for p in range(1, count):
                body(p)
        else:
            def wrapped(p, carry):
                body(p)
                return carry
            lax.fori_loop(1, count, wrapped, 0)

    def greet(p):
        pl.semaphore_signal(barrier, inc=1, device_id=peer(p), device_id_type=MESH)

    over_peers(greet)

    places = []
    for q in range(9):
        if q != 4:
            dx, dy = q // 3 - 1, q % 3 - 1
            there = (gx + dx >= 0) & (gx + dx < along) & (gy + dy >= 0) & (gy + dy < across)
            places.append((q, there, (gx + dx, gy + dy)))

    def halo(buf, send, recv):
        def copy(q, device):
            return pltpu.make_async_remote_copy(
                src_ref=buf.at[4], dst_ref=buf.at[8 - q], send_sem=send.at[q],
                recv_sem=recv.at[8 - q], device_id=device, device_id_type=MESH,
            )

        def arrive(q, device):
            return pltpu.make_async_remote_copy(
                src_ref=buf.at[4], dst_ref=buf.at[q], send_sem=send.at[q],
                recv_sem=recv.at[q], device_id=device, device_id_type=MESH,
            )

        def start():
            for q, there, device in places:
                pl.when(there)(lambda q=q, device=device: copy(q, device).start())

        def wait_recv():
            for q, there, device in places:
                pl.when(there)(lambda q=q, device=device: arrive(q, device).wait_recv())

        def wait_send():
            for q, there, device in places:
                pl.when(there)(lambda q=q, device=device: copy(q, device).wait_send())

        return start, wait_recv, wait_send

    def localize(ids):
        owner = jnp.right_shift(ids, log_rows)
        ox = jnp.right_shift(owner, log_across) - gx + 1
        oy = jnp.bitwise_and(owner, across - 1) - gy + 1
        inside = (ids >= 0) & (ox >= 0) & (ox < 3) & (oy >= 0) & (oy < 3)
        row = jnp.bitwise_and(ids, nrows - 1)
        spot = jnp.where(row >= half, wrows - half, 0) + (ox * 3 + oy) * half + row
        return jnp.where(inside, spot, -1)

    load_nb.wait()
    own = nb_ref[...]
    own_t = jnp.transpose(own)
    tab[4, 0:slots, :] = jnp.concatenate([own_t] * (128 // nrows), axis=1)

    spots = localize(own)
    lanes2 = iota((nrows, wrows), 1)
    n_even = jnp.zeros((nrows, wrows), F32)
    n_odd = jnp.zeros((nrows, wrows), F32)
    for k in range(slots):
        col = spots[:, k:k + 1]
        n_even = jnp.where(col == lanes2, 1.0, n_even)
        n_odd = jnp.where(col == lanes2 + wrows, 1.0, n_odd)
    a4[2 * nrows:3 * nrows, :] = n_even.astype(BF16)
    a4[3 * nrows:4 * nrows, :] = n_odd.astype(BF16)

    load_vb.wait()
    vb = vb_ref[...] - gx * (across * nrows)
    vrow = jnp.bitwise_and(vb, nrows - 1)
    code = (
        jnp.where(vrow >= half, across * half - half, 0)
        + jnp.right_shift(vb, log_rows) * half + vrow
    )
    for g in range(across * nrows // 16):
        block = iota((16, vb.shape[1]), 0) + 16 * g
        onehot[16 * g:16 * (g + 1), :] = jnp.where(block == code, 1.0, 0.0).astype(BF16)

    nwin[...] = jnp.zeros(nwin.shape, BF16)
    for g in range(3 * nrows // 16):
        shape = (16, nrows * 128)
        spread_sel[16 * g:16 * (g + 1), :] = jnp.where(
            jnp.right_shift(iota(shape, 1), 7) == iota(shape, 0) + 16 * g % nrows, 1.0, 0.0
        ).astype(BF16)

    pl.semaphore_wait(barrier, count - 1)
    tab_start, tab_wait, tab_done = halo(tab, tab_send, tab_recv)
    tab_start()

    load_b.wait()
    lane = iota((width, 128), 1)

    def reduce_coeff(b, rows, acc):
        prod = f_ref[b] * rows
        part = prod[:, 0:128]
        for j in range(1, prod.shape[1] // 128):
            part = part + prod[:, j * 128:(j + 1) * 128]
        total = jnp.sum(part, axis=1, keepdims=True)
        h, i = b // half, b % half
        acc[h] = jnp.where(lane == i, total, acc[h])

    def pack(acc):
        both = jnp.concatenate(acc, axis=0)
        return jnp.transpose(both)[0:half, :]

    acc = [jnp.zeros((width, 128), F32)] * 2
    for c in range(CHUNKS):
        load_f[c].wait()
        for b in range(c * step, (c + 1) * step):
            reduce_coeff(b, b_ref[b:b + 1, :], acc)
    win[0, 4] = pack(acc)
    win_ops = [halo(win.at[k], win_send.at[k], win_recv.at[k]) for k in range(ITERS)]
    win_ops[0][0]()

    tab_wait()
    group = iota((slots, 128), 1) // nrows
    for ox in range(3):
        ids = jnp.where(
            group == 0, tab[3 * ox, 0:slots, :],
            jnp.where(group == 1, tab[3 * ox + 1, 0:slots, :], tab[3 * ox + 2, 0:slots, :]),
        )
        target = jnp.where(group < 3, localize(ids), -1)
        target = (target - wrows).astype(F32)
        rows = [
            jnp.broadcast_to(target[k:k + 1, :], (16, 128)).astype(BF16) for k in range(slots)
        ]
        low, high = ((0, 6), (0, 9), (3, 9))[ox]
        per = (high - low) * half // 16

        def build(g, carry, rows=rows, low=low, per=per, ox=ox):
            h = g // per
            start = pl.multiple_of(h * wrows + low * half + (g - h * per) * 16, 16)
            spot = (iota((16, 128), 0) + (start - wrows)).astype(F32).astype(BF16)
            hits = jnp.zeros((16, 128), BF16)
            for row in rows:
                hits = jnp.where(row == spot, jnp.ones((16, 128), BF16), hits)
            nwin[pl.ds(start, 16), ox * 128:(ox + 1) * 128] = hits
            return carry

        lax.fori_loop(0, 2 * per, build, 0)
    n_loc = jnp.concatenate(
        [nwin[4 * half:5 * half, :], nwin[wrows + 4 * half:wrows + 5 * half, :]], axis=0
    )
    for h in range(2):
        two = lax.dot_general(
            n_loc, nwin[h * wrows:(h + 1) * wrows, :], (((1,), (1,)), ((), ())),
            preferred_element_type=F32,
        )
        a4[h * nrows:(h + 1) * nrows, :] = two.astype(BF16)
    load_d.wait()

    low_lanes = iota((nrows, 128), 1) < width
    ar_rows = iota((8, 128), 0)
    ar_lanes = iota((8, 128), 1)

    def fold(x):
        tot = x[0:8, :]
        for i in range(1, x.shape[0] // 8):
            tot = tot + x[8 * i:8 * (i + 1), :]
        res = tot[:, 0:128]
        for j in range(1, x.shape[1] // 128):
            res = res + tot[:, 128 * j:128 * (j + 1)]
        return jnp.sum(res, axis=0, keepdims=True)

    def send(buf, own, send_sem, recv_sem, device):
        pltpu.make_async_remote_copy(
            src_ref=buf.at[it, own], dst_ref=buf.at[it, own], send_sem=send_sem.at[it],
            recv_sem=recv_sem.at[it], device_id=device, device_id_type=MESH,
        ).start()

    def landed(buf, k, sem, number):
        part = buf.at[k, pl.ds(0, number)]
        pltpu.make_async_copy(part, part, sem.at[k]).wait()

    sub = iota((8, 128), 0)

    def fold8(v):
        one = []
        for i in range(4):
            t = jnp.where(sub < 4, v[i], v[i + 4])
            u = jnp.where(sub < 4, v[i + 4], v[i])
            one.append(t + pltpu.roll(u, 4, 0))
        two = [
            jnp.where(
                sub % 4 < 2, one[i] + pltpu.roll(one[i], 6, 0),
                one[i + 2] + pltpu.roll(one[i + 2], 2, 0),
            )
            for i in range(2)
        ]
        return jnp.where(
            sub % 2 == 0, two[0] + pltpu.roll(two[0], 7, 0), two[1] + pltpu.roll(two[1], 1, 0)
        )

    r = b_ref[...]
    beta = None
    firsts = []
    alphas, betas = [], []
    for it in range(ITERS):
        dr = d_ref[...] * r
        dr_ref[...] = dr
        gamma_part = fold(r * r)
        delta_part = fold(r * dr)
        mu_part = fold(r * s_ref[...]) if it else jnp.zeros((1, 128), F32)
        if it == 0:
            win_ops[0][1]()
            cr = win[0].reshape(wrows, 2 * width)
        parts = jnp.concatenate(split3(cr), axis=1)
        prod = jnp.dot(a4[...], parts, preferred_element_type=F32)
        prod = prod[:, 0:128] + prod[:, 128:256] + prod[:, 256:384]
        second = prod[0:nrows] + pltpu.roll(prod[nrows:2 * nrows], width, 1)
        first = prod[2 * nrows:3 * nrows] + pltpu.roll(prod[3 * nrows:], width, 1)
        delta_part = delta_part + fold(jnp.where(low_lanes, first * first, 0.0))
        three = jnp.where(
            ar_rows == 0, gamma_part, jnp.where(ar_rows == 1, delta_part, mu_part)
        )
        three = jnp.sum(three, axis=1, keepdims=True)
        sums[it, me] = jnp.sum(
            jnp.where((ar_rows == ar_lanes) & (ar_rows < 3), three, 0.0), axis=0, keepdims=True
        )

        over_peers(lambda p: send(sums, me, sum_send, sum_recv, peer(p)))

        slab[it, gy] = jnp.where(
            low_lanes[0:half], first[0:half], pltpu.roll(first[half:], width, 1)
        )
        for device in row_peers:
            send(slab, gy, slab_send, slab_recv, device)

        thirds = jnp.concatenate([t.astype(F32) for t in split3(second)], axis=0)
        thirds = jnp.transpose(thirds)[0:width, :].astype(BF16)
        for c in range(0, nrows * 128, 512):
            rep[:, c:c + 512] = jnp.dot(
                thirds, spread_sel[:, c:c + 512], preferred_element_type=F32
            )
        acc = [jnp.zeros((width, 128), F32)] * 2
        for g in range(0, nrows, 8):
            tiles = f_ref.shape[2] // 128
            parts = [[None] * 8 for _ in range(tiles)]
            for b in range(8):
                factor = rep[:, (g + b) * 128:(g + b + 1) * 128]
                for j in range(tiles):
                    prod = f_ref[g + b, :, j * 128:(j + 1) * 128] * factor
                    parts[j][b] = jnp.sum(prod.reshape(width // 8, 8, 128), axis=0)
            image = jnp.concatenate([fold8(part) for part in parts], axis=1)
            w_ref[g:g + 8, :] = dr_ref[g:g + 8, :] + image
            if it < ITERS - 1:
                for b in range(g, g + 8):
                    reduce_coeff(b, w_ref[b:b + 1, :], acc)
        if it < ITERS - 1:
            win[it + 1, 4] = pack(acc)
            win_ops[it + 1][0]()
        else:
            load_vf.wait()
            for k in range(ITERS):
                landed(slab, k, slab_recv, across - 1)
            pieces = [slab[k].reshape(across * half, 2 * width) for k in range(ITERS)]
            old = pieces[1] + betas[1] * pieces[0]
            known = alphas[0] * pieces[0] + alphas[1] * old
            vert = []
            for piece in (known, pieces[2], old):
                turned = jnp.transpose(piece)
                turned = jnp.concatenate([turned[0:width], turned[width:]], axis=1)
                hi = turned.astype(BF16)
                lo = (turned - hi.astype(F32)).astype(BF16)
                both = jnp.dot(
                    jnp.concatenate([hi, lo], axis=0), onehot[...], preferred_element_type=F32
                )
                vert.append(jnp.sum(
                    (both[0:width] + both[width:]) * vf_ref[...], axis=0, keepdims=True
                ))

        landed(sums, it, sum_recv, count - 1)
        total = jnp.sum(sums[it], axis=0)
        gamma, delta, mu = total[:, 0:1], total[:, 1:2], total[:, 2:3]
        if it == 0:
            energy = delta
        else:
            beta = gamma / gamma_old
            energy = delta + beta * (2.0 * mu + beta * energy)
        alpha = gamma / energy
        gamma_old = gamma
        alphas.append(alpha)
        betas.append(beta)
        if it < ITERS - 1:
            win_ops[it + 1][1]()
            cw = win[it + 1].reshape(wrows, 2 * width)
            cs = cw if it == 0 else cw + beta * cs
            cr = cr - alpha * cs
        w = w_ref[...]
        if it == 0:
            p, s = r, w
            x = alpha * p
        else:
            p = r + beta * p_ref[...]
            s = w + beta * s_ref[...]
            x = x_ref[...] + alpha * p
        r = r - alpha * s
        x_ref[...] = x
        if it < ITERS - 1:
            p_ref[...] = p
            s_ref[...] = s
    r_ref[...] = r
    out_ref[...] = vert[0] + alphas[2] * (vert[1] + betas[2] * vert[2])


    tab_done()
    for it in range(ITERS):
        win_ops[it][2]()
        landed(sums, it, sum_send, count - 1)
        landed(slab, it, slab_send, across - 1)


def finish(x_in, r_in, v_in, x_out, r_out, v_out, sems):
    copies = [
        pltpu.make_async_copy(a, b, sems.at[i])
        for i, (a, b) in enumerate(((x_in, x_out), (r_in, r_out), (v_in, v_out)))
    ]
    for copy in copies:
        copy.start()
    for copy in copies:
        copy.wait()


def per_device(right_side, diagonal, features, neighbours, vertex_features, vertex_bricks):
    nrows, width, vox = features.shape
    slots = neighbours.shape[1]
    verts = vertex_bricks.shape[0]
    along, across = lax.axis_size("gx"), lax.axis_size("gy")
    count = along * across
    half = nrows // 2
    vmem = pl.BlockSpec(memory_space=pltpu.VMEM)
    hbm = pl.BlockSpec(memory_space=pltpu.HBM)
    field = jax.ShapeDtypeStruct((nrows, vox), F32)
    x, r, out = pl.pallas_call(
        functools.partial(kernel, along, across, nrows, width, slots),
        out_shape=(field, field, jax.ShapeDtypeStruct((1, verts), F32)),
        in_specs=[hbm] * 6,
        out_specs=[vmem] * 3,
        scratch_shapes=[
            pltpu.VMEM((nrows, vox), F32),
            pltpu.VMEM((nrows, vox), F32),
            pltpu.VMEM((nrows, width, vox), F32),
            pltpu.VMEM((nrows, slots), jnp.int32),
            pltpu.VMEM((width, verts), F32),
            pltpu.VMEM((1, verts), jnp.int32),
            pltpu.VMEM((nrows, vox), F32),
            pltpu.VMEM((nrows, vox), F32),
            pltpu.VMEM((nrows, vox), F32),
            pltpu.VMEM((nrows, vox), F32),
            pltpu.VMEM((9, 32, 128), jnp.int32),
            pltpu.VMEM((ITERS, 9, half, 2 * width), F32),
            pltpu.VMEM((ITERS, across, half, 2 * width), F32),
            pltpu.VMEM((ITERS, count, 1, 128), F32),
            pltpu.VMEM((9 * nrows, 384), BF16),
            pltpu.VMEM((4 * nrows, 9 * half), BF16),
            pltpu.VMEM((across * nrows, verts), BF16),
            pltpu.VMEM((3 * nrows, nrows * 128), BF16),
            pltpu.VMEM((width, nrows * 128), F32),
            pltpu.SemaphoreType.DMA((5 + CHUNKS,)),
            pltpu.SemaphoreType.DMA((9,)),
            pltpu.SemaphoreType.DMA((9,)),
            pltpu.SemaphoreType.DMA((ITERS, 9)),
            pltpu.SemaphoreType.DMA((ITERS, 9)),
            pltpu.SemaphoreType.DMA((ITERS,)),
            pltpu.SemaphoreType.DMA((ITERS,)),
            pltpu.SemaphoreType.DMA((ITERS,)),
            pltpu.SemaphoreType.DMA((ITERS,)),
        ],
        compiler_params=pltpu.CompilerParams(
            collective_id=0, has_side_effects=True, vmem_limit_bytes=VMEM_BYTES
        ),
    )(right_side, diagonal, features, neighbours, vertex_features, vertex_bricks.reshape(1, verts))
    x, r, out = pl.pallas_call(
        finish,
        out_shape=(field, field, jax.ShapeDtypeStruct((1, verts), F32)),
        in_specs=[vmem] * 3,
        out_specs=[hbm] * 3,
        scratch_shapes=[pltpu.SemaphoreType.DMA((3,))],
        compiler_params=pltpu.CompilerParams(vmem_limit_bytes=VMEM_BYTES),
    )(x, r, out)
    return x, r, out.reshape(verts)


def solution(mesh):
    rows = P(("gx", "gy"), None)
    placed = (rows, rows, P(("gx", "gy"), None, None), rows, P(None, ("gx", "gy")), P(("gx", "gy")))
    return jax.shard_map(
        per_device,
        mesh=mesh,
        in_specs=placed,
        out_specs=(rows, rows, P(("gx", "gy"))),
        check_vma=False,
    )
```

```python
import functools

import jax
import jax.numpy as jnp
from jax import lax
from jax.experimental import pallas as pl
from jax.experimental.pallas import tpu as pltpu
from jax.sharding import PartitionSpec as P

ITERS = 3
CHUNKS = 4
VMEM_BYTES = 40 * 1024 * 1024
MESH = pl.DeviceIdType.MESH
F32 = jnp.float32
BF16 = jnp.bfloat16


def split3(x):
    hi = x.astype(BF16)
    rest = x - hi.astype(F32)
    mid = rest.astype(BF16)
    lo = (rest - mid.astype(F32)).astype(BF16)
    return hi, mid, lo


def iota(shape, dim):
    return lax.broadcasted_iota(jnp.int32, shape, dim)


def kernel(
    along, across, nrows, width, slots,
    b_hbm, d_hbm, f_hbm, nb_hbm, vf_hbm, vb_hbm,
    x_ref, r_ref, out_ref,
    b_ref, d_ref, f_ref, nb_ref, vf_ref, vb_ref, dr_ref, p_ref, s_ref, w_ref,
    tab, win, slab, sums, nwin, a4, onehot, spread_sel, rep, lane_sel, part_hi, part_lo,
    load_sem, tab_send, tab_recv, win_send, win_recv, slab_send, slab_recv,
    sum_send, sum_recv,
):
    half = nrows // 2
    wrows = 9 * half
    count = along * across
    gx = lax.axis_index("gx")
    gy = lax.axis_index("gy")
    me = gx * across + gy
    log_rows = nrows.bit_length() - 1
    log_across = across.bit_length() - 1

    step = nrows // CHUNKS
    load_b = pltpu.make_async_copy(b_hbm, b_ref, load_sem.at[0])
    load_d = pltpu.make_async_copy(d_hbm, d_ref, load_sem.at[1])
    load_vf = pltpu.make_async_copy(vf_hbm, vf_ref, load_sem.at[2])
    load_f = [
        pltpu.make_async_copy(
            f_hbm.at[pl.ds(c * step, step)], f_ref.at[pl.ds(c * step, step)], load_sem.at[5 + c]
        )
        for c in range(CHUNKS)
    ]
    load_nb = pltpu.make_async_copy(nb_hbm, nb_ref, load_sem.at[3])
    load_vb = pltpu.make_async_copy(vb_hbm, vb_ref, load_sem.at[4])
    load_nb.start()
    load_b.start()
    load_vb.start()
    for copy in load_f:
        copy.start()
    load_d.start()
    load_vf.start()

    tab[...] = jnp.full(tab.shape, -1, jnp.int32)
    win[...] = jnp.zeros(win.shape, F32)

    barrier = pltpu.get_barrier_semaphore()
    row_peers = [(gx, lax.rem(gy + p, across)) for p in range(1, across)]

    def peer(p):
        dev = lax.rem(me + p, count)
        return (dev // across, lax.rem(dev, across))

    def over_peers(body):
        if count <= 32:
            for p in range(1, count):
                body(p)
        else:
            def wrapped(p, carry):
                body(p)
                return carry
            lax.fori_loop(1, count, wrapped, 0)

    def greet(p):
        pl.semaphore_signal(barrier, inc=1, device_id=peer(p), device_id_type=MESH)

    over_peers(greet)

    places = []
    for q in range(9):
        if q != 4:
            dx, dy = q // 3 - 1, q % 3 - 1
            there = (gx + dx >= 0) & (gx + dx < along) & (gy + dy >= 0) & (gy + dy < across)
            places.append((q, there, (gx + dx, gy + dy)))

    def halo(buf, send, recv):
        def copy(q, device):
            return pltpu.make_async_remote_copy(
                src_ref=buf.at[4], dst_ref=buf.at[8 - q], send_sem=send.at[q],
                recv_sem=recv.at[8 - q], device_id=device, device_id_type=MESH,
            )

        def arrive(q, device):
            return pltpu.make_async_remote_copy(
                src_ref=buf.at[4], dst_ref=buf.at[q], send_sem=send.at[q],
                recv_sem=recv.at[q], device_id=device, device_id_type=MESH,
            )

        def start():
            for q, there, device in places:
                pl.when(there)(lambda q=q, device=device: copy(q, device).start())

        def wait_recv():
            for q, there, device in places:
                pl.when(there)(lambda q=q, device=device: arrive(q, device).wait_recv())

        def wait_send():
            for q, there, device in places:
                pl.when(there)(lambda q=q, device=device: copy(q, device).wait_send())

        return start, wait_recv, wait_send

    def localize(ids):
        owner = jnp.right_shift(ids, log_rows)
        ox = jnp.right_shift(owner, log_across) - gx + 1
        oy = jnp.bitwise_and(owner, across - 1) - gy + 1
        inside = (ids >= 0) & (ox >= 0) & (ox < 3) & (oy >= 0) & (oy < 3)
        row = jnp.bitwise_and(ids, nrows - 1)
        spot = jnp.where(row >= half, wrows - half, 0) + (ox * 3 + oy) * half + row
        return jnp.where(inside, spot, -1)

    load_nb.wait()
    own = nb_ref[...]
    own_t = jnp.transpose(own)
    tab[4, 0:slots, :] = jnp.concatenate([own_t] * (128 // nrows), axis=1)

    spots = localize(own)
    lanes2 = iota((nrows, wrows), 1)
    n_even = jnp.zeros((nrows, wrows), F32)
    n_odd = jnp.zeros((nrows, wrows), F32)
    for k in range(slots):
        col = spots[:, k:k + 1]
        n_even = jnp.where(col == lanes2, 1.0, n_even)
        n_odd = jnp.where(col == lanes2 + wrows, 1.0, n_odd)
    a4[2 * nrows:3 * nrows, :] = n_even.astype(BF16)
    a4[3 * nrows:4 * nrows, :] = n_odd.astype(BF16)

    load_vb.wait()
    vb = vb_ref[...] - gx * (across * nrows)
    vrow = jnp.bitwise_and(vb, nrows - 1)
    code = (
        jnp.where(vrow >= half, across * half - half, 0)
        + jnp.right_shift(vb, log_rows) * half + vrow
    )
    for g in range(across * nrows // 16):
        block = iota((16, vb.shape[1]), 0) + 16 * g
        onehot[16 * g:16 * (g + 1), :] = jnp.where(block == code, 1.0, 0.0).astype(BF16)

    nwin[...] = jnp.zeros(nwin.shape, BF16)
    shape = (128, 128)
    for i in range(half):
        lane_sel[i * 128:(i + 1) * 128, :] = jnp.where(iota(shape, 1) == i, 1.0, 0.0).astype(BF16)
    for g in range(3 * nrows // 16):
        shape = (16, nrows * 128)
        spread_sel[16 * g:16 * (g + 1), :] = jnp.where(
            jnp.right_shift(iota(shape, 1), 7) == iota(shape, 0) + 16 * g % nrows, 1.0, 0.0
        ).astype(BF16)

    pl.semaphore_wait(barrier, count - 1)
    tab_start, tab_wait, tab_done = halo(tab, tab_send, tab_recv)
    tab_start()

    load_b.wait()

    def reduce_coeff(b, rows):
        prod = f_ref[b] * rows
        part = prod[:, 0:128]
        for j in range(1, prod.shape[1] // 128):
            part = part + prod[:, j * 128:(j + 1) * 128]
        hi = part.astype(BF16)
        part_hi[:, b * 128:(b + 1) * 128] = hi
        part_lo[:, b * 128:(b + 1) * 128] = (part - hi.astype(F32)).astype(BF16)

    def pack():
        both = []
        for h in range(2):
            span = slice(h * half * 128, (h + 1) * half * 128)
            both.append(
                jnp.dot(part_hi[:, span], lane_sel[...], preferred_element_type=F32)
                + jnp.dot(part_lo[:, span], lane_sel[...], preferred_element_type=F32)
            )
        return jnp.transpose(jnp.concatenate(both, axis=0))[0:half, :]

    for c in range(CHUNKS):
        load_f[c].wait()
        for b in range(c * step, (c + 1) * step):
            reduce_coeff(b, b_ref[b:b + 1, :])
    win[0, 4] = pack()
    win_ops = [halo(win.at[k], win_send.at[k], win_recv.at[k]) for k in range(ITERS)]
    win_ops[0][0]()

    tab_wait()
    group = iota((slots, 128), 1) // nrows
    for ox in range(3):
        ids = jnp.where(
            group == 0, tab[3 * ox, 0:slots, :],
            jnp.where(group == 1, tab[3 * ox + 1, 0:slots, :], tab[3 * ox + 2, 0:slots, :]),
        )
        target = jnp.where(group < 3, localize(ids), -1)
        target = (target - wrows).astype(F32)
        rows = [
            jnp.broadcast_to(target[k:k + 1, :], (16, 128)).astype(BF16) for k in range(slots)
        ]
        low, high = ((0, 6), (0, 9), (3, 9))[ox]
        per = (high - low) * half // 16

        def build(g, carry, rows=rows, low=low, per=per, ox=ox):
            h = g // per
            start = pl.multiple_of(h * wrows + low * half + (g - h * per) * 16, 16)
            spot = (iota((16, 128), 0) + (start - wrows)).astype(F32).astype(BF16)
            hits = jnp.zeros((16, 128), BF16)
            for row in rows:
                hits = jnp.where(row == spot, jnp.ones((16, 128), BF16), hits)
            nwin[pl.ds(start, 16), ox * 128:(ox + 1) * 128] = hits
            return carry

        lax.fori_loop(0, 2 * per, build, 0)
    n_loc = jnp.concatenate(
        [nwin[4 * half:5 * half, :], nwin[wrows + 4 * half:wrows + 5 * half, :]], axis=0
    )
    for h in range(2):
        two = lax.dot_general(
            n_loc, nwin[h * wrows:(h + 1) * wrows, :], (((1,), (1,)), ((), ())),
            preferred_element_type=F32,
        )
        a4[h * nrows:(h + 1) * nrows, :] = two.astype(BF16)
    load_d.wait()

    low_lanes = iota((nrows, 128), 1) < width
    ar_rows = iota((8, 128), 0)
    ar_lanes = iota((8, 128), 1)

    def fold(x):
        tot = x[0:8, :]
        for i in range(1, x.shape[0] // 8):
            tot = tot + x[8 * i:8 * (i + 1), :]
        res = tot[:, 0:128]
        for j in range(1, x.shape[1] // 128):
            res = res + tot[:, 128 * j:128 * (j + 1)]
        return jnp.sum(res, axis=0, keepdims=True)

    def send(buf, own, send_sem, recv_sem, device):
        pltpu.make_async_remote_copy(
            src_ref=buf.at[it, own], dst_ref=buf.at[it, own], send_sem=send_sem.at[it],
            recv_sem=recv_sem.at[it], device_id=device, device_id_type=MESH,
        ).start()

    def landed(buf, k, sem, number):
        part = buf.at[k, pl.ds(0, number)]
        pltpu.make_async_copy(part, part, sem.at[k]).wait()

    sub = iota((8, 128), 0)

    def fold8(v):
        one = []
        for i in range(4):
            t = jnp.where(sub < 4, v[i], v[i + 4])
            u = jnp.where(sub < 4, v[i + 4], v[i])
            one.append(t + pltpu.roll(u, 4, 0))
        two = [
            jnp.where(
                sub % 4 < 2, one[i] + pltpu.roll(one[i], 6, 0),
                one[i + 2] + pltpu.roll(one[i + 2], 2, 0),
            )
            for i in range(2)
        ]
        return jnp.where(
            sub % 2 == 0, two[0] + pltpu.roll(two[0], 7, 0), two[1] + pltpu.roll(two[1], 1, 0)
        )

    r = b_ref[...]
    beta = None
    firsts = []
    alphas, betas = [], []
    for it in range(ITERS):
        dr = d_ref[...] * r
        dr_ref[...] = dr
        gamma_part = fold(r * r)
        delta_part = fold(r * dr)
        mu_part = fold(r * s_ref[...]) if it else jnp.zeros((1, 128), F32)
        if it == 0:
            win_ops[0][1]()
            cr = win[0].reshape(wrows, 2 * width)
        parts = jnp.concatenate(split3(cr), axis=1)
        prod = jnp.dot(a4[...], parts, preferred_element_type=F32)
        prod = prod[:, 0:128] + prod[:, 128:256] + prod[:, 256:384]
        second = prod[0:nrows] + pltpu.roll(prod[nrows:2 * nrows], width, 1)
        first = prod[2 * nrows:3 * nrows] + pltpu.roll(prod[3 * nrows:], width, 1)
        delta_part = delta_part + fold(jnp.where(low_lanes, first * first, 0.0))
        three = jnp.where(
            ar_rows == 0, gamma_part, jnp.where(ar_rows == 1, delta_part, mu_part)
        )
        three = jnp.sum(three, axis=1, keepdims=True)
        sums[it, me] = jnp.sum(
            jnp.where((ar_rows == ar_lanes) & (ar_rows < 3), three, 0.0), axis=0, keepdims=True
        )

        over_peers(lambda p: send(sums, me, sum_send, sum_recv, peer(p)))

        slab[it, gy] = jnp.where(
            low_lanes[0:half], first[0:half], pltpu.roll(first[half:], width, 1)
        )
        for device in row_peers:
            send(slab, gy, slab_send, slab_recv, device)

        thirds = jnp.concatenate([t.astype(F32) for t in split3(second)], axis=0)
        thirds = jnp.transpose(thirds)[0:width, :].astype(BF16)
        for c in range(0, nrows * 128, 512):
            rep[:, c:c + 512] = jnp.dot(
                thirds, spread_sel[:, c:c + 512], preferred_element_type=F32
            )
        for g in range(0, nrows, 8):
            tiles = f_ref.shape[2] // 128
            parts = [[None] * 8 for _ in range(tiles)]
            for b in range(8):
                factor = rep[:, (g + b) * 128:(g + b + 1) * 128]
                for j in range(tiles):
                    prod = f_ref[g + b, :, j * 128:(j + 1) * 128] * factor
                    parts[j][b] = jnp.sum(prod.reshape(width // 8, 8, 128), axis=0)
            image = jnp.concatenate([fold8(part) for part in parts], axis=1)
            w_ref[g:g + 8, :] = dr_ref[g:g + 8, :] + image
            if it < ITERS - 1:
                for b in range(g, g + 8):
                    reduce_coeff(b, w_ref[b:b + 1, :])
        if it < ITERS - 1:
            win[it + 1, 4] = pack()
            win_ops[it + 1][0]()
        else:
            load_vf.wait()
            for k in range(ITERS):
                landed(slab, k, slab_recv, across - 1)
            pieces = [slab[k].reshape(across * half, 2 * width) for k in range(ITERS)]
            old = pieces[1] + betas[1] * pieces[0]
            known = alphas[0] * pieces[0] + alphas[1] * old
            vert = []
            for piece in (known, pieces[2], old):
                turned = jnp.transpose(piece)
                turned = jnp.concatenate([turned[0:width], turned[width:]], axis=1)
                hi = turned.astype(BF16)
                lo = (turned - hi.astype(F32)).astype(BF16)
                both = jnp.dot(
                    jnp.concatenate([hi, lo], axis=0), onehot[...], preferred_element_type=F32
                )
                vert.append(jnp.sum(
                    (both[0:width] + both[width:]) * vf_ref[...], axis=0, keepdims=True
                ))

        landed(sums, it, sum_recv, count - 1)
        total = jnp.sum(sums[it], axis=0)
        gamma, delta, mu = total[:, 0:1], total[:, 1:2], total[:, 2:3]
        if it == 0:
            energy = delta
        else:
            beta = gamma / gamma_old
            energy = delta + beta * (2.0 * mu + beta * energy)
        alpha = gamma / energy
        gamma_old = gamma
        alphas.append(alpha)
        betas.append(beta)
        if it < ITERS - 1:
            win_ops[it + 1][1]()
            cw = win[it + 1].reshape(wrows, 2 * width)
            cs = cw if it == 0 else cw + beta * cs
            cr = cr - alpha * cs
        w = w_ref[...]
        if it == 0:
            p, s = r, w
            x = alpha * p
        else:
            p = r + beta * p_ref[...]
            s = w + beta * s_ref[...]
            x = x_ref[...] + alpha * p
        r = r - alpha * s
        x_ref[...] = x
        if it < ITERS - 1:
            p_ref[...] = p
            s_ref[...] = s
    r_ref[...] = r
    out_ref[...] = vert[0] + alphas[2] * (vert[1] + betas[2] * vert[2])


    tab_done()
    for it in range(ITERS):
        win_ops[it][2]()
        landed(sums, it, sum_send, count - 1)
        landed(slab, it, slab_send, across - 1)


def finish(x_in, r_in, v_in, x_out, r_out, v_out, sems):
    copies = [
        pltpu.make_async_copy(a, b, sems.at[i])
        for i, (a, b) in enumerate(((x_in, x_out), (r_in, r_out), (v_in, v_out)))
    ]
    for copy in copies:
        copy.start()
    for copy in copies:
        copy.wait()


def per_device(right_side, diagonal, features, neighbours, vertex_features, vertex_bricks):
    nrows, width, vox = features.shape
    slots = neighbours.shape[1]
    verts = vertex_bricks.shape[0]
    along, across = lax.axis_size("gx"), lax.axis_size("gy")
    count = along * across
    half = nrows // 2
    vmem = pl.BlockSpec(memory_space=pltpu.VMEM)
    hbm = pl.BlockSpec(memory_space=pltpu.HBM)
    field = jax.ShapeDtypeStruct((nrows, vox), F32)
    x, r, out = pl.pallas_call(
        functools.partial(kernel, along, across, nrows, width, slots),
        out_shape=(field, field, jax.ShapeDtypeStruct((1, verts), F32)),
        in_specs=[hbm] * 6,
        out_specs=[vmem] * 3,
        scratch_shapes=[
            pltpu.VMEM((nrows, vox), F32),
            pltpu.VMEM((nrows, vox), F32),
            pltpu.VMEM((nrows, width, vox), F32),
            pltpu.VMEM((nrows, slots), jnp.int32),
            pltpu.VMEM((width, verts), F32),
            pltpu.VMEM((1, verts), jnp.int32),
            pltpu.VMEM((nrows, vox), F32),
            pltpu.VMEM((nrows, vox), F32),
            pltpu.VMEM((nrows, vox), F32),
            pltpu.VMEM((nrows, vox), F32),
            pltpu.VMEM((9, 32, 128), jnp.int32),
            pltpu.VMEM((ITERS, 9, half, 2 * width), F32),
            pltpu.VMEM((ITERS, across, half, 2 * width), F32),
            pltpu.VMEM((ITERS, count, 1, 128), F32),
            pltpu.VMEM((9 * nrows, 384), BF16),
            pltpu.VMEM((4 * nrows, 9 * half), BF16),
            pltpu.VMEM((across * nrows, verts), BF16),
            pltpu.VMEM((3 * nrows, nrows * 128), BF16),
            pltpu.VMEM((width, nrows * 128), F32),
            pltpu.VMEM((half * 128, 128), BF16),
            pltpu.VMEM((width, nrows * 128), BF16),
            pltpu.VMEM((width, nrows * 128), BF16),
            pltpu.SemaphoreType.DMA((5 + CHUNKS,)),
            pltpu.SemaphoreType.DMA((9,)),
            pltpu.SemaphoreType.DMA((9,)),
            pltpu.SemaphoreType.DMA((ITERS, 9)),
            pltpu.SemaphoreType.DMA((ITERS, 9)),
            pltpu.SemaphoreType.DMA((ITERS,)),
            pltpu.SemaphoreType.DMA((ITERS,)),
            pltpu.SemaphoreType.DMA((ITERS,)),
            pltpu.SemaphoreType.DMA((ITERS,)),
        ],
        compiler_params=pltpu.CompilerParams(
            collective_id=0, has_side_effects=True, vmem_limit_bytes=VMEM_BYTES
        ),
    )(*[
        pltpu.with_memory_space_constraint(a, pltpu.HBM)
        for a in (
            right_side, diagonal, features, neighbours, vertex_features,
            vertex_bricks.reshape(1, verts),
        )
    ])
    x, r, out = pl.pallas_call(
        finish,
        out_shape=(field, field, jax.ShapeDtypeStruct((1, verts), F32)),
        in_specs=[vmem] * 3,
        out_specs=[hbm] * 3,
        scratch_shapes=[pltpu.SemaphoreType.DMA((3,))],
        compiler_params=pltpu.CompilerParams(vmem_limit_bytes=VMEM_BYTES),
    )(x, r, out)
    return x, r, out.reshape(verts)


def solution(mesh):
    rows = P(("gx", "gy"), None)
    placed = (rows, rows, P(("gx", "gy"), None, None), rows, P(None, ("gx", "gy")), P(("gx", "gy")))
    return jax.shard_map(
        per_device,
        mesh=mesh,
        in_specs=placed,
        out_specs=(rows, rows, P(("gx", "gy"))),
        check_vma=False,
    )
```

```python
import functools

import jax
import jax.numpy as jnp
from jax import lax
from jax.experimental import pallas as pl
from jax.experimental.pallas import tpu as pltpu
from jax.sharding import PartitionSpec as P

ITERS = 3
CHUNKS = 4
VMEM_BYTES = 40 * 1024 * 1024
MESH = pl.DeviceIdType.MESH
F32 = jnp.float32
BF16 = jnp.bfloat16


def split3(x):
    hi = x.astype(BF16)
    rest = x - hi.astype(F32)
    mid = rest.astype(BF16)
    lo = (rest - mid.astype(F32)).astype(BF16)
    return hi, mid, lo


def iota(shape, dim):
    return lax.broadcasted_iota(jnp.int32, shape, dim)


def kernel(
    along, across, nrows, width, slots,
    b_hbm, d_hbm, f_hbm, nb_hbm, vf_hbm, vb_hbm,
    x_ref, r_ref, out_ref,
    b_ref, d_ref, f_ref, nb_ref, vf_ref, vb_ref, dr_ref, p_ref, s_ref, w_ref,
    tab, win, slab, sums, nwin, a4, onehot, spread_sel, rep,
    load_sem, tab_send, tab_recv, win_send, win_recv, slab_send, slab_recv,
    sum_send, sum_recv,
):
    half = nrows // 2
    wrows = 9 * half
    count = along * across
    gx = lax.axis_index("gx")
    gy = lax.axis_index("gy")
    me = gx * across + gy
    log_rows = nrows.bit_length() - 1
    log_across = across.bit_length() - 1

    step = nrows // CHUNKS
    load_b = pltpu.make_async_copy(b_hbm, b_ref, load_sem.at[0])
    load_d = pltpu.make_async_copy(d_hbm, d_ref, load_sem.at[1])
    load_vf = pltpu.make_async_copy(vf_hbm, vf_ref, load_sem.at[2])
    load_f = [
        pltpu.make_async_copy(
            f_hbm.at[pl.ds(c * step, step)], f_ref.at[pl.ds(c * step, step)], load_sem.at[5 + c]
        )
        for c in range(CHUNKS)
    ]
    load_nb = pltpu.make_async_copy(nb_hbm, nb_ref, load_sem.at[3])
    load_vb = pltpu.make_async_copy(vb_hbm, vb_ref, load_sem.at[4])
    load_nb.start()
    load_b.start()
    load_vb.start()
    for copy in load_f:
        copy.start()
    load_d.start()
    load_vf.start()

    tab[...] = jnp.full(tab.shape, -1, jnp.int32)
    win[...] = jnp.zeros(win.shape, F32)

    barrier = pltpu.get_barrier_semaphore()
    row_peers = [(gx, lax.rem(gy + p, across)) for p in range(1, across)]

    def peer(p):
        dev = lax.rem(me + p, count)
        return (dev // across, lax.rem(dev, across))

    def over_peers(body):
        if count <= 32:
            for p in range(1, count):
                body(p)
        else:
            def wrapped(p, carry):
                body(p)
                return carry
            lax.fori_loop(1, count, wrapped, 0)

    def greet(p):
        pl.semaphore_signal(barrier, inc=1, device_id=peer(p), device_id_type=MESH)

    over_peers(greet)

    places = []
    for q in range(9):
        if q != 4:
            dx, dy = q // 3 - 1, q % 3 - 1
            there = (gx + dx >= 0) & (gx + dx < along) & (gy + dy >= 0) & (gy + dy < across)
            places.append((q, there, (gx + dx, gy + dy)))

    def halo(buf, send, recv):
        def copy(q, device):
            return pltpu.make_async_remote_copy(
                src_ref=buf.at[4], dst_ref=buf.at[8 - q], send_sem=send.at[q],
                recv_sem=recv.at[8 - q], device_id=device, device_id_type=MESH,
            )

        def arrive(q, device):
            return pltpu.make_async_remote_copy(
                src_ref=buf.at[4], dst_ref=buf.at[q], send_sem=send.at[q],
                recv_sem=recv.at[q], device_id=device, device_id_type=MESH,
            )

        def start():
            for q, there, device in places:
                pl.when(there)(lambda q=q, device=device: copy(q, device).start())

        def wait_recv():
            for q, there, device in places:
                pl.when(there)(lambda q=q, device=device: arrive(q, device).wait_recv())

        def wait_send():
            for q, there, device in places:
                pl.when(there)(lambda q=q, device=device: copy(q, device).wait_send())

        return start, wait_recv, wait_send

    def localize(ids):
        owner = jnp.right_shift(ids, log_rows)
        ox = jnp.right_shift(owner, log_across) - gx + 1
        oy = jnp.bitwise_and(owner, across - 1) - gy + 1
        inside = (ids >= 0) & (ox >= 0) & (ox < 3) & (oy >= 0) & (oy < 3)
        row = jnp.bitwise_and(ids, nrows - 1)
        spot = jnp.where(row >= half, wrows - half, 0) + (ox * 3 + oy) * half + row
        return jnp.where(inside, spot, -1)

    load_nb.wait()
    own = nb_ref[...]
    own_t = jnp.transpose(own)
    tab[4, 0:slots, :] = jnp.concatenate([own_t] * (128 // nrows), axis=1)

    spots = localize(own)
    lanes2 = iota((nrows, wrows), 1)
    n_even = jnp.zeros((nrows, wrows), F32)
    n_odd = jnp.zeros((nrows, wrows), F32)
    for k in range(slots):
        col = spots[:, k:k + 1]
        n_even = jnp.where(col == lanes2, 1.0, n_even)
        n_odd = jnp.where(col == lanes2 + wrows, 1.0, n_odd)
    a4[2 * nrows:3 * nrows, :] = n_even.astype(BF16)
    a4[3 * nrows:4 * nrows, :] = n_odd.astype(BF16)

    load_vb.wait()
    vb = vb_ref[...] - gx * (across * nrows)
    vrow = jnp.bitwise_and(vb, nrows - 1)
    code = (
        jnp.where(vrow >= half, across * half - half, 0)
        + jnp.right_shift(vb, log_rows) * half + vrow
    )
    for g in range(across * nrows // 16):
        block = iota((16, vb.shape[1]), 0) + 16 * g
        onehot[16 * g:16 * (g + 1), :] = jnp.where(block == code, 1.0, 0.0).astype(BF16)

    nwin[...] = jnp.zeros(nwin.shape, BF16)
    for g in range(3 * nrows // 16):
        shape = (16, nrows * 128)
        spread_sel[16 * g:16 * (g + 1), :] = jnp.where(
            jnp.right_shift(iota(shape, 1), 7) == iota(shape, 0) + 16 * g % nrows, 1.0, 0.0
        ).astype(BF16)

    pl.semaphore_wait(barrier, count - 1)
    tab_start, tab_wait, tab_done = halo(tab, tab_send, tab_recv)
    tab_start()

    load_b.wait()
    lane = iota((width, 128), 1)

    def reduce_coeff(b, rows, acc):
        prod = f_ref[b] * rows
        part = prod[:, 0:128]
        for j in range(1, prod.shape[1] // 128):
            part = part + prod[:, j * 128:(j + 1) * 128]
        total = jnp.sum(part, axis=1, keepdims=True)
        h, i = b // half, b % half
        acc[h] = jnp.where(lane == i, total, acc[h])

    def pack(acc):
        both = jnp.concatenate(acc, axis=0)
        return jnp.transpose(both)[0:half, :]

    acc = [jnp.zeros((width, 128), F32)] * 2
    for c in range(CHUNKS):
        load_f[c].wait()
        for b in range(c * step, (c + 1) * step):
            reduce_coeff(b, b_ref[b:b + 1, :], acc)
    win[0, 4] = pack(acc)
    win_ops = [halo(win.at[k], win_send.at[k], win_recv.at[k]) for k in range(ITERS)]
    win_ops[0][0]()

    tab_wait()
    group = iota((slots, 128), 1) // nrows
    for ox in range(3):
        ids = jnp.where(
            group == 0, tab[3 * ox, 0:slots, :],
            jnp.where(group == 1, tab[3 * ox + 1, 0:slots, :], tab[3 * ox + 2, 0:slots, :]),
        )
        target = jnp.where(group < 3, localize(ids), -1)
        target = (target - wrows).astype(F32)
        rows = [
            jnp.broadcast_to(target[k:k + 1, :], (16, 128)).astype(BF16) for k in range(slots)
        ]
        low, high = ((0, 6), (0, 9), (3, 9))[ox]
        per = (high - low) * half // 16

        def build(g, carry, rows=rows, low=low, per=per, ox=ox):
            h = g // per
            start = pl.multiple_of(h * wrows + low * half + (g - h * per) * 16, 16)
            spot = (iota((16, 128), 0) + (start - wrows)).astype(F32).astype(BF16)
            hits = jnp.zeros((16, 128), BF16)
            for row in rows:
                hits = jnp.where(row == spot, jnp.ones((16, 128), BF16), hits)
            nwin[pl.ds(start, 16), ox * 128:(ox + 1) * 128] = hits
            return carry

        lax.fori_loop(0, 2 * per, build, 0)
    n_loc = jnp.concatenate(
        [nwin[4 * half:5 * half, :], nwin[wrows + 4 * half:wrows + 5 * half, :]], axis=0
    )
    for h in range(2):
        two = lax.dot_general(
            n_loc, nwin[h * wrows:(h + 1) * wrows, :], (((1,), (1,)), ((), ())),
            preferred_element_type=F32,
        )
        a4[h * nrows:(h + 1) * nrows, :] = two.astype(BF16)
    load_d.wait()

    low_lanes = iota((nrows, 128), 1) < width
    ar_rows = iota((8, 128), 0)
    ar_lanes = iota((8, 128), 1)

    def fold(x):
        tot = x[0:8, :]
        for i in range(1, x.shape[0] // 8):
            tot = tot + x[8 * i:8 * (i + 1), :]
        res = tot[:, 0:128]
        for j in range(1, x.shape[1] // 128):
            res = res + tot[:, 128 * j:128 * (j + 1)]
        return jnp.sum(res, axis=0, keepdims=True)

    def send(buf, own, send_sem, recv_sem, device):
        pltpu.make_async_remote_copy(
            src_ref=buf.at[it, own], dst_ref=buf.at[it, own], send_sem=send_sem.at[it],
            recv_sem=recv_sem.at[it], device_id=device, device_id_type=MESH,
        ).start()

    def landed(buf, k, sem, number):
        part = buf.at[k, pl.ds(0, number)]
        pltpu.make_async_copy(part, part, sem.at[k]).wait()

    sub = iota((8, 128), 0)

    def fold8(v):
        one = []
        for i in range(4):
            t = jnp.where(sub < 4, v[i], v[i + 4])
            u = jnp.where(sub < 4, v[i + 4], v[i])
            one.append(t + pltpu.roll(u, 4, 0))
        two = [
            jnp.where(
                sub % 4 < 2, one[i] + pltpu.roll(one[i], 6, 0),
                one[i + 2] + pltpu.roll(one[i + 2], 2, 0),
            )
            for i in range(2)
        ]
        return jnp.where(
            sub % 2 == 0, two[0] + pltpu.roll(two[0], 7, 0), two[1] + pltpu.roll(two[1], 1, 0)
        )

    r = b_ref[...]
    beta = None
    firsts = []
    alphas, betas = [], []
    for it in range(ITERS):
        dr = d_ref[...] * r
        dr_ref[...] = dr
        gamma_part = fold(r * r)
        delta_part = fold(r * dr)
        mu_part = fold(r * s_ref[...]) if it else jnp.zeros((1, 128), F32)
        if it == 0:
            win_ops[0][1]()
            cr = win[0].reshape(wrows, 2 * width)
        parts = jnp.concatenate(split3(cr), axis=1)
        prod = jnp.dot(a4[...], parts, preferred_element_type=F32)
        prod = prod[:, 0:128] + prod[:, 128:256] + prod[:, 256:384]
        second = prod[0:nrows] + pltpu.roll(prod[nrows:2 * nrows], width, 1)
        first = prod[2 * nrows:3 * nrows] + pltpu.roll(prod[3 * nrows:], width, 1)
        delta_part = delta_part + fold(jnp.where(low_lanes, first * first, 0.0))
        three = jnp.where(
            ar_rows == 0, gamma_part, jnp.where(ar_rows == 1, delta_part, mu_part)
        )
        three = jnp.sum(three, axis=1, keepdims=True)
        sums[it, me] = jnp.sum(
            jnp.where((ar_rows == ar_lanes) & (ar_rows < 3), three, 0.0), axis=0, keepdims=True
        )

        over_peers(lambda p: send(sums, me, sum_send, sum_recv, peer(p)))

        slab[it, gy] = jnp.where(
            low_lanes[0:half], first[0:half], pltpu.roll(first[half:], width, 1)
        )
        for device in row_peers:
            send(slab, gy, slab_send, slab_recv, device)

        thirds = jnp.concatenate([t.astype(F32) for t in split3(second)], axis=0)
        thirds = jnp.transpose(thirds)[0:width, :].astype(BF16)
        for c in range(0, nrows * 128, 512):
            rep[:, c:c + 512] = jnp.dot(
                thirds, spread_sel[:, c:c + 512], preferred_element_type=F32
            )
        acc = [jnp.zeros((width, 128), F32)] * 2
        for g in range(0, nrows, 8):
            tiles = f_ref.shape[2] // 128
            parts = [[None] * 8 for _ in range(tiles)]
            for b in range(8):
                factor = rep[:, (g + b) * 128:(g + b + 1) * 128]
                for j in range(tiles):
                    prod = f_ref[g + b, :, j * 128:(j + 1) * 128] * factor
                    parts[j][b] = jnp.sum(prod.reshape(width // 8, 8, 128), axis=0)
            image = jnp.concatenate([fold8(part) for part in parts], axis=1)
            w_ref[g:g + 8, :] = dr_ref[g:g + 8, :] + image
            if it < ITERS - 1:
                for b in range(g, g + 8):
                    reduce_coeff(b, w_ref[b:b + 1, :], acc)
        if it < ITERS - 1:
            win[it + 1, 4] = pack(acc)
            win_ops[it + 1][0]()
        else:
            load_vf.wait()
            for k in range(ITERS):
                landed(slab, k, slab_recv, across - 1)
            pieces = [slab[k].reshape(across * half, 2 * width) for k in range(ITERS)]
            old = pieces[1] + betas[1] * pieces[0]
            known = alphas[0] * pieces[0] + alphas[1] * old
            vert = []
            for piece in (known, pieces[2], old):
                turned = jnp.transpose(piece)
                turned = jnp.concatenate([turned[0:width], turned[width:]], axis=1)
                hi = turned.astype(BF16)
                lo = (turned - hi.astype(F32)).astype(BF16)
                both = jnp.dot(
                    jnp.concatenate([hi, lo], axis=0), onehot[...], preferred_element_type=F32
                )
                vert.append(jnp.sum(
                    (both[0:width] + both[width:]) * vf_ref[...], axis=0, keepdims=True
                ))

        landed(sums, it, sum_recv, count - 1)
        total = jnp.sum(sums[it], axis=0)
        gamma, delta, mu = total[:, 0:1], total[:, 1:2], total[:, 2:3]
        if it == 0:
            energy = delta
        else:
            beta = gamma / gamma_old
            energy = delta + beta * (2.0 * mu + beta * energy)
        alpha = gamma / energy
        gamma_old = gamma
        alphas.append(alpha)
        betas.append(beta)
        if it < ITERS - 1:
            win_ops[it + 1][1]()
            cw = win[it + 1].reshape(wrows, 2 * width)
            cs = cw if it == 0 else cw + beta * cs
            cr = cr - alpha * cs
        w = w_ref[...]
        if it == 0:
            p, s = r, w
            x = alpha * p
        else:
            p = r + beta * p_ref[...]
            s = w + beta * s_ref[...]
            x = x_ref[...] + alpha * p
        r = r - alpha * s
        x_ref[...] = x
        if it < ITERS - 1:
            p_ref[...] = p
            s_ref[...] = s
    r_ref[...] = r
    out_ref[...] = vert[0] + alphas[2] * (vert[1] + betas[2] * vert[2])


    tab_done()
    for it in range(ITERS):
        win_ops[it][2]()
        landed(sums, it, sum_send, count - 1)
        landed(slab, it, slab_send, across - 1)


def finish(x_in, r_in, v_in, x_out, r_out, v_out, sems):
    copies = [
        pltpu.make_async_copy(a, b, sems.at[i])
        for i, (a, b) in enumerate(((x_in, x_out), (r_in, r_out), (v_in, v_out)))
    ]
    for copy in copies:
        copy.start()
    for copy in copies:
        copy.wait()


def per_device(right_side, diagonal, features, neighbours, vertex_features, vertex_bricks):
    nrows, width, vox = features.shape
    slots = neighbours.shape[1]
    verts = vertex_bricks.shape[0]
    along, across = lax.axis_size("gx"), lax.axis_size("gy")
    count = along * across
    half = nrows // 2
    vmem = pl.BlockSpec(memory_space=pltpu.VMEM)
    hbm = pl.BlockSpec(memory_space=pltpu.HBM)
    field = jax.ShapeDtypeStruct((nrows, vox), F32)
    x, r, out = pl.pallas_call(
        functools.partial(kernel, along, across, nrows, width, slots),
        out_shape=(field, field, jax.ShapeDtypeStruct((1, verts), F32)),
        in_specs=[hbm] * 6,
        out_specs=[vmem] * 3,
        scratch_shapes=[
            pltpu.VMEM((nrows, vox), F32),
            pltpu.VMEM((nrows, vox), F32),
            pltpu.VMEM((nrows, width, vox), F32),
            pltpu.VMEM((nrows, slots), jnp.int32),
            pltpu.VMEM((width, verts), F32),
            pltpu.VMEM((1, verts), jnp.int32),
            pltpu.VMEM((nrows, vox), F32),
            pltpu.VMEM((nrows, vox), F32),
            pltpu.VMEM((nrows, vox), F32),
            pltpu.VMEM((nrows, vox), F32),
            pltpu.VMEM((9, 32, 128), jnp.int32),
            pltpu.VMEM((ITERS, 9, half, 2 * width), F32),
            pltpu.VMEM((ITERS, across, half, 2 * width), F32),
            pltpu.VMEM((ITERS, count, 1, 128), F32),
            pltpu.VMEM((9 * nrows, 384), BF16),
            pltpu.VMEM((4 * nrows, 9 * half), BF16),
            pltpu.VMEM((across * nrows, verts), BF16),
            pltpu.VMEM((3 * nrows, nrows * 128), BF16),
            pltpu.VMEM((width, nrows * 128), F32),
            pltpu.SemaphoreType.DMA((5 + CHUNKS,)),
            pltpu.SemaphoreType.DMA((9,)),
            pltpu.SemaphoreType.DMA((9,)),
            pltpu.SemaphoreType.DMA((ITERS, 9)),
            pltpu.SemaphoreType.DMA((ITERS, 9)),
            pltpu.SemaphoreType.DMA((ITERS,)),
            pltpu.SemaphoreType.DMA((ITERS,)),
            pltpu.SemaphoreType.DMA((ITERS,)),
            pltpu.SemaphoreType.DMA((ITERS,)),
        ],
        compiler_params=pltpu.CompilerParams(
            collective_id=0, has_side_effects=True, vmem_limit_bytes=VMEM_BYTES
        ),
    )(*[
        pltpu.with_memory_space_constraint(a, pltpu.HBM)
        for a in (
            right_side, diagonal, features, neighbours, vertex_features,
            vertex_bricks.reshape(1, verts),
        )
    ])
    x, r, out = pl.pallas_call(
        finish,
        out_shape=(field, field, jax.ShapeDtypeStruct((1, verts), F32)),
        in_specs=[vmem] * 3,
        out_specs=[hbm] * 3,
        scratch_shapes=[pltpu.SemaphoreType.DMA((3,))],
        compiler_params=pltpu.CompilerParams(vmem_limit_bytes=VMEM_BYTES),
    )(x, r, out)
    return x, r, out.reshape(verts)


def solution(mesh):
    rows = P(("gx", "gy"), None)
    placed = (rows, rows, P(("gx", "gy"), None, None), rows, P(None, ("gx", "gy")), P(("gx", "gy")))
    return jax.shard_map(
        per_device,
        mesh=mesh,
        in_specs=placed,
        out_specs=(rows, rows, P(("gx", "gy"))),
        check_vma=False,
    )
```
